128 devices in a mesh: dp: 16 (over y_hi, z, core), seq: 8 (over y_lo, x).
Axes of the slice: x: 4, y: 4 (y_hi: 2, y_lo: 2; y = y_hi * 2 + y_lo), z: 4, core: 2. Of those that a mesh axis runs over, the one named last changes fastest.
Arguments:
- packed_bases: int32 [16, 2048], P('dp', 'seq'), may hold values from 0 to 1073741823
- rc_flags: int32 [16], P('dp'), may hold values 0 or 1
- shifts: int32 [16], P('dp'), may hold values from -3 to 3
- cotangent: bfloat16 [16, 15360, 608], P('dp', 'seq'), may hold values from -0.015625 to 0.015625
- stem_weight: bfloat16 [15, 4, 512], replicated, may hold values from -0.75 to 0.75
- pool_gain: float32 [512], replicated, may hold values from 0.5 to 8
- tower_weight: bfloat16 [608, 5, 512], replicated, may hold values from -0.125 to 0.125
Outputs:
- response: bfloat16 [16, 15360, 608], P('dp', 'seq')
- stem_grad: float32 [15, 4, 512], replicated
- gain_grad: float32 [512], replicated
- tower_grad: float32 [608, 5, 512], P('dp')
The draws below stay inside these ranges and needn't reach their ends.
All inputs are finite; a program needn't handle non-finite values. No bound on the sum of `rc_flags` on one device may be relied on, other than what follows from the above.
Results may differ from the reference program's by a relative error of at most 0.0075.
Values may be sent and summed in bfloat16 or wider, within the bound.
A program may use at most 192 MiB of HBM per device.

```python
import math
import jax
import jax.numpy as jnp
from jax import lax

C1 = 512
F2 = 608
K1 = 15
K2 = 5
WINDOWS = 16
WORDS = 2048
POOLED = 15360


def with_ends(drawn, key, low, top_value):
    longest = drawn.shape.index(max(drawn.shape))
    spots = []
    for shift in (0, 1):
        where = [jax.random.randint(jax.random.fold_in(key, axis), (), 0, length) for axis, length in enumerate(drawn.shape)]
        where[longest] = (where[longest] + shift) % drawn.shape[longest]
        spots.append(tuple(where))
    return drawn.at[spots[0]].set(low).at[spots[1]].set(top_value)


def with_spikes(values, key, source, target, blocks, factor):
    owner, partner = [(jnp.arange(values.shape[axis_at]) // (values.shape[axis_at] // blocks)).reshape([-1 if axis == axis_at else 1 for axis in range(values.ndim)]) for axis_at in (source, target)]
    chosen = jax.random.permutation(key, blocks)[partner]
    strong = (owner == chosen) | (owner == (partner + blocks // 2) % blocks)
    return jnp.where(strong, factor * values, values)


def levels(stream_key, dims, pieces, low, largest):
    def one(position, parts):
        steps = jax.random.uniform(jax.random.fold_in(jax.random.fold_in(stream_key, 6), position), (parts,), jnp.float32, low / len(pieces), largest / len(pieces))
        return jnp.repeat(jnp.exp(steps), dims[position] // parts).reshape((-1,) + (1,) * (len(dims) - position - 1))

    factor_of = one(*pieces[0])
    for cut in pieces[1:]:
        factor_of = factor_of * one(*cut)
    return factor_of


def bell_draw(own_key, dims, spread, most, cuts=(), held_as=jnp.bfloat16):
    values = jax.random.normal(own_key, dims, jnp.float32) * spread
    if len(cuts) > 0:
        values = levels(own_key, dims, cuts, -0.22, 0.18) * values
    return jnp.clip(values, min=-most, max=most).astype(held_as)


def bell_draw_with(rng, extent, width, limit, split, heavy, held_as=jnp.bfloat16):
    result = width * jax.random.normal(rng, extent, jnp.float32)
    if split:
        result = result * levels(rng, extent, split, -0.22, 0.18)
    return jnp.clip(with_spikes(result, jax.random.fold_in(rng, 3), *heavy), -limit, limit).astype(held_as)


def setup_inputs(seed: int = 0) -> dict:
    splits = jax.random.split(jax.random.key(seed), 8)
    return {
        "packed_bases": with_ends(jax.random.randint(splits[0], (WINDOWS, WORDS), 0, 1073741824), jax.random.fold_in(splits[0], 1), 0, 1073741823).astype(jnp.int32),
        "rc_flags": with_ends((jax.random.randint(splits[1], (WINDOWS,), 0, 2) < 1).astype(jnp.int32), jax.random.fold_in(splits[1], 1), 0, 1),
        "shifts": with_ends(jax.random.randint(splits[2], (WINDOWS,), -3, 4), jax.random.fold_in(splits[2], 1), -3, 3).astype(jnp.int32),
        "cotangent": bell_draw_with(splits[3], (WINDOWS, POOLED, F2), ((WINDOWS * POOLED) ** -0.5), 0.015625, ((0, 16), (1, 8)), (0, 2, 16, 2.0)),
        "stem_weight": bell_draw(splits[4], (K1, 4, C1), (4 * K1) ** -0.5, 0.75),
        "pool_gain": jnp.clip(jnp.exp(jax.random.uniform(splits[5], (C1,), jnp.float32, math.log(0.5), math.log(8.0))), 0.5, 8.0),
        "tower_weight": bell_draw(splits[6], (F2, K2, C1), (K2 * C1) ** -0.5, 0.125),
    }


def decode(packed):
    powers = jnp.array([4 ** i for i in range(15)], dtype=jnp.int32)
    return (packed[:, None] // powers[None, :] % 4).reshape(-1).astype(jnp.int32)

def onehot_columns(symbols, row_count):
    letters = jnp.arange(4, dtype=jnp.int32)
    onehot = (symbols[:, None] == letters[None, :]).astype(jnp.bfloat16)
    return jnp.stack([onehot[tap_index:tap_index + row_count] for tap_index in range(K1)], axis=1).reshape(row_count, 4 * K1)

def pool_forward(stem_out, pool_gain):
    pairs = stem_out.reshape(stem_out.shape[0] // 2, 2, stem_out.shape[1])
    even_rows = pairs[:, 0]
    odd_rows = pairs[:, 1]
    pair_diff = even_rows - odd_rows
    pair_weight = jax.nn.sigmoid(pool_gain[None, :] * pair_diff)
    return (odd_rows + pair_weight * pair_diff, pair_diff, pair_weight)

def pool_backward(pool_grad, pair_diff, pair_weight, pool_gain):
    slope = pair_weight * (1.0 - pair_weight)
    diff_grad = pool_grad * (pair_weight + pool_gain[None, :] * pair_diff * slope)
    gain_part = lax.optimization_barrier(jnp.sum(pool_grad * pair_diff * pair_diff * slope, axis=0))
    stem_out_grad = jnp.stack([diff_grad, pool_grad - diff_grad], axis=1).reshape(-1, pool_grad.shape[1])
    return (stem_out_grad, gain_part)

def window(packed, rc_flag, shift_by, cot_rows, stem_weight, pool_gain, tower_weight):
    total_len = packed.shape[0] * 15
    base_ids = decode(packed)
    augmented = jnp.where(rc_flag == 1, 3 - base_ids[::-1], base_ids)
    global_pos = jnp.arange(total_len + 14, dtype=jnp.int32) - 7 - shift_by
    in_range = (global_pos >= 0) & (global_pos < total_len)
    symbols = jnp.where(in_range, augmented[jnp.clip(global_pos, 0, total_len - 1)], -1)
    columns = onehot_columns(symbols, total_len)
    stem_out = jnp.dot(columns, stem_weight.reshape(4 * K1, C1), preferred_element_type=jnp.float32)
    pooled, pair_diff, pair_weight = pool_forward(stem_out, pool_gain)
    activated = jax.nn.gelu(pooled, approximate=True).astype(jnp.bfloat16)
    row_count = total_len // 2
    half = K2 // 2
    padded = jnp.pad(activated, ((half, half), (0, 0)))
    padded_grad = jnp.pad(cot_rows, ((half, half), (0, 0)))
    response = jnp.zeros((row_count, F2), jnp.float32)
    act_grad = jnp.zeros((row_count, C1), jnp.float32)
    tap_grads = []
    for tap_index in range(K2):
        shifted = padded[tap_index:tap_index + row_count]
        response = response + lax.dot_general(shifted, tower_weight[:, tap_index, :], (((1,), (1,)), ((), ())), preferred_element_type=jnp.float32)
        tap_grads.append(lax.dot_general(cot_rows, shifted, (((0,), (0,)), ((), ())), preferred_element_type=jnp.float32))
        start = 2 * half - tap_index
        act_grad = act_grad + jnp.dot(padded_grad[start:start + row_count], tower_weight[:, tap_index, :], preferred_element_type=jnp.float32)
    tower_grad = jnp.stack(tap_grads, axis=1)
    act_grad = act_grad.astype(jnp.bfloat16)
    _, pullback = jax.vjp(lambda value: jax.nn.gelu(value, approximate=True), pooled)
    pool_grad = pullback(act_grad.astype(jnp.float32))[0]
    stem_out_grad, gain_part = pool_backward(pool_grad, pair_diff, pair_weight, pool_gain)
    stem_part = jnp.dot(columns.astype(jnp.float32).T, stem_out_grad, precision=lax.Precision.HIGHEST)
    return (response.astype(jnp.bfloat16), stem_part.reshape(K1, 4, C1), gain_part, tower_grad)

def reference(packed_bases, rc_flags, shifts, cotangent, stem_weight, pool_gain, tower_weight):

    def one_window(items):
        return window(items[0], items[1], items[2], items[3], stem_weight, pool_gain, tower_weight)
    results = lax.map(one_window, (packed_bases, rc_flags, shifts, cotangent))
    return (results[0], lax.optimization_barrier(jnp.sum(results[1], axis=0)), lax.optimization_barrier(jnp.sum(results[2], axis=0)), lax.optimization_barrier(jnp.sum(results[3], axis=0)))
```

```python
import functools
import jax
import jax.numpy as jnp
from jax import lax
from jax.experimental import pallas as pl
from jax.experimental.pallas import tpu as pltpu
from jax.sharding import PartitionSpec as P

F32, BF16, I32 = jnp.float32, jnp.bfloat16, jnp.int32
C1, F2, K1, K2 = 512, 608, 15, 5
ROWS = 1920
WIDE = 2048
KF = 3072
UNIT = 768
SEQ = 8
CH = 256


def dot(a, b):
    return lax.dot_general(a, b, (((1,), (0,)), ((), ())), preferred_element_type=F32)


def dot_nt(a, b):
    return lax.dot_general(a, b, (((1,), (1,)), ((), ())), preferred_element_type=F32)


def prep_stem_weight(sw_ref, sw_f, wcat, gain, gain_b):
    sw_f[60:64, 0:C1] = jnp.zeros((4, C1), F32)
    sw_f[0:4, C1:] = jnp.zeros((4, C1), F32)
    for s in range(K1):
        v = sw_ref[s].astype(F32)
        sw_f[4 * s : 4 * s + 4, 0:C1] = v
        sw_f[4 * s + 4 : 4 * s + 8, C1:] = v
    wcat[...] = sw_f[...].T.astype(BF16)
    gain_b[...] = jnp.broadcast_to(gain[...], (128, C1)).T


def prep_tower_weight(w5, wt):
    flat = w5.reshape(K2 * F2, C1)

    def block(i, _):
        r0 = pl.multiple_of(i * 128, 128)
        wt[:, pl.ds(r0, 128)] = flat[pl.ds(r0, 128), :].T
        return 0

    lax.fori_loop(0, (K2 * F2) // 128, block, 0)
    tail = K2 * F2 - (K2 * F2) // 128 * 128
    v = jnp.concatenate([flat[K2 * F2 - tail :, :], jnp.zeros((128 - tail, C1), BF16)], axis=0)
    wt[:, KF - 128 :] = v.T


def prep_cot(cot_v, halo, seq, gt):
    lane = lax.broadcasted_iota(I32, (16, 128), 1)

    def rows(i, _):
        r0 = pl.multiple_of(i * 16, 16)
        rs = pl.ds(r0, 16)
        nxt = jnp.where(seq < SEQ - 1, halo[1, rs, :].astype(F32), 0.0)
        prv = jnp.where(seq > 0, halo[0, rs, :].astype(F32), 0.0)
        rim = jnp.where(lane < 64, nxt, prv).astype(BF16)
        full = jnp.concatenate([cot_v[rs, :], rim], axis=1)
        for t in range(K2):
            s = 2 - t
            v = full if s == 0 else pltpu.roll(full, (-s) % WIDE, 1)
            gt[pl.ds(pl.multiple_of(t * F2 + r0, 16), 16), :] = v[:, 0:ROWS]
        return 0

    lax.fori_loop(0, F2 // 16, rows, 0)
    gt[K2 * F2 : KF, :] = jnp.zeros((KF - K2 * F2, ROWS), BF16)


def decode(words, rc, shift, seq, oh):
    take = jnp.where(rc == 1, SEQ - 1 - seq, seq)
    slot = lax.broadcasted_iota(I32, (SEQ, 1, CH), 0)
    w8 = words[...]
    own = jnp.sum(jnp.where(slot == take, w8, 0), axis=0)
    low = jnp.sum(jnp.where(slot == take - 1, w8, 0), axis=0)
    high = jnp.sum(jnp.where(slot == take + 1, w8, 0), axis=0)
    lane = lax.broadcasted_iota(I32, (1, 128), 1)
    rim = jnp.where(lane == 127, low[:, 128:256], jnp.where(lane == 0, high[:, 0:128], 0))
    row = jnp.broadcast_to(jnp.concatenate([own, rim], axis=1), (8, 384))
    after = jnp.where(rc == 1, pltpu.roll(row, 1, 1), pltpu.roll(row, 383, 1))
    sub = lax.broadcasted_iota(I32, (8, 384), 0)
    planes = (jnp.where(sub < 4, row, after) >> (8 * (sub & 3))) & 255
    planes = planes.astype(F32).astype(BF16)
    src = lax.broadcasted_iota(I32, (384, CH), 0)
    src = jnp.where(src == 383, -1, src)
    part = lax.broadcasted_iota(I32, (64, CH), 0)
    s = part >> 2
    want = jnp.where(rc == 1, 3 - (part & 3), part & 3)

    def chunk(i, _):
        u0 = pl.multiple_of(i * CH, CH)
        u = u0 + lax.broadcasted_iota(I32, (1, CH), 1)
        q = jnp.where(u < 1984, u, u - WIDE)
        b0 = 2 * q - 7 - shift
        j0 = (((b0 + 30) * 34953) >> 19) - 2
        i0 = b0 - 15 * j0
        at = jnp.where(rc == 1, 255 - j0, j0)
        sel = jnp.where(src == at, 1.0, 0.0).astype(BF16)
        got = dot(planes, sel).astype(I32)
        word_a = got[0:1] + (got[1:2] << 8) + (got[2:3] << 16) + (got[3:4] << 24)
        word_b = got[4:5] + (got[5:6] << 8) + (got[6:7] << 16) + (got[7:8] << 24)
        d = i0 + s
        late = d >= 15
        word = jnp.where(late, word_b, word_a)
        d = jnp.where(late, d - 15, d)
        d = jnp.where(rc == 1, 14 - d, d)
        where = 2 * ROWS * seq + b0 + s
        good = (where >= 0) & (where < 2 * ROWS * SEQ)
        hit = (((word >> (2 * d)) & 3) == want) & good
        oh[:, pl.ds(u0, CH)] = jnp.where(hit, 1.0, 0.0).astype(BF16)
        return 0

    lax.fori_loop(0, WIDE // CH, chunk, 0)


GELU_A = 0.7978845608028654
GELU_B = 0.044715


def forward(even, odd, gain):
    diff = even - odd
    weight = 0.5 * jnp.tanh((0.5 * gain) * diff) + 0.5
    x = odd + weight * diff
    x2 = x * x
    th = jnp.tanh(x * (GELU_A + (GELU_A * GELU_B) * x2))
    hx = 0.5 * x
    act = hx + hx * th
    return diff, weight, x2, th, hx, act


def slopes(gain, diff, weight, x2, th, hx):
    slope = weight - weight * weight
    dgelu = (0.5 + 0.5 * th) + hx * (1.0 - th * th) * (GELU_A + (3 * GELU_A * GELU_B) * x2)
    m1 = weight + gain * diff * slope
    m2 = diff * diff * slope
    return dgelu, m1, m2


def main_loop(oh, wcat, gain_b, seq, gt, wt, stem_s, ag_s, sg_s, act, gain_acc, stem_acc):
    gain_acc[...] = jnp.zeros_like(gain_acc)
    stem_acc[...] = jnp.zeros_like(stem_acc)

    def tile(n, lt, rows, rows2, u0, back):
        cols = slice(lt * 128, lt * 128 + 128)
        gain = gain_b[rows, :]
        diff, weight, x2, th, hx, a = forward(stem_s[rows, cols], stem_s[rows2, cols], gain)
        if not back:
            lane = lax.broadcasted_iota(I32, (16, 128), 1)
            out = ((lane < 64) & (seq == SEQ - 1)) | ((lane >= 64) & (seq == 0))
            a = jnp.where(out, 0.0, a)
        act[rows, pl.ds(pl.multiple_of(u0 + lt * 128, 128), 128)] = a.astype(BF16)
        if back:
            dgelu, m1, m2 = slopes(gain, diff, weight, x2, th, hx)
            pg = ag_s[rows, cols].astype(BF16).astype(F32) * dgelu
            dg = pg * m1
            sg_s[rows, cols] = dg.astype(BF16)
            sg_s[rows2, cols] = (pg - dg).astype(BF16)
            gain_acc[rows, :] += pg * m2

    def step(u0, width):
        us = pl.ds(u0, CH)
        stem_s[...] = dot(wcat[...], oh[:, us])
        ag_s[:, 0:width] = dot(wt[...], gt[:, pl.ds(u0, width)])

        def chunk(i, _):
            r0 = pl.multiple_of(i * 16, 16)
            rows = pl.ds(r0, 16)
            rows2 = pl.ds(pl.multiple_of(C1 + r0, 16), 16)
            for lt in range(2):
                tile(0, lt, rows, rows2, u0, lt * 128 < width)
            return 0

        lax.fori_loop(0, C1 // 16, chunk, 0, unroll=2)
        stem_acc[...] += dot_nt(sg_s[:, 0:width], oh[:, pl.ds(u0, width)])

    def group(g, _):
        step(pl.multiple_of(g * CH, CH), CH)
        return 0

    lax.fori_loop(0, 7, group, 0)
    step(7 * CH, 128)


def shift_act(act, xt):
    def rows(i, _):
        r0 = pl.multiple_of(i * 16, 16)
        full = act[pl.ds(r0, 16), :]
        for t in range(K2):
            s = t - 2
            v = full if s == 0 else pltpu.roll(full, (-s) % WIDE, 1)
            xt[pl.ds(pl.multiple_of(t * C1 + r0, 16), 16), :] = v[:, 0:ROWS]
        return 0

    lax.fori_loop(0, C1 // 16, rows, 0)


def tower_part(cot_v, xt, tg_s, unit_s):
    def tap(t, _):
        tg_s[...] = dot_nt(cot_v[...], xt[pl.ds(pl.multiple_of(t * C1, C1), C1), :])
        for d in range(16):
            for ct in range(4):
                piece = tg_s[38 * d : 38 * d + 38, ct * 128 : (ct + 1) * 128]
                unit_s[d, pl.ds(152 * t + 38 * ct, 38), :] = piece
        return 0

    lax.fori_loop(0, K2, tap, 0)
    for d in range(16):
        unit_s[d, 760:768, :] = jnp.zeros((8, 128), F32)


def response_step(xt, w5, resp_v, u0, width):
    taps = jnp.concatenate([w5[t] for t in range(K2)], axis=1)
    cols = pl.ds(u0, width)
    resp_v[:, cols] = dot(taps, xt[:, cols]).astype(BF16)


ORDER = ((0, 1, 2), (1, 2, 0), (2, 0, 1))
MESH = pl.DeviceIdType.MESH


def device_at(x, y, z, core):
    return ((y // 2) * 8 + z * 2 + core, (y % 2) * 4 + x)


def send(src, dst, ssem, rsem, to):
    return pltpu.make_async_remote_copy(
        src_ref=src, dst_ref=dst, send_sem=ssem, recv_sem=rsem, device_id=to, device_id_type=MESH
    )


def greet(me):
    barrier = pltpu.get_barrier_semaphore()
    x, y, z, core = me
    peers = []
    for dx in range(4):
        for dy in range(4):
            for dz in range(4):
                if (dx, dy, dz) != (0, 0, 0) and 0 in (dx, dy, dz):
                    peers.append(device_at((x + dx) % 4, (y + dy) % 4, (z + dz) % 4, core))
    for dz in range(4):
        peers.append(device_at(x, y, (z + dz) % 4, 1 - core))
    for peer in peers:
        pl.semaphore_signal(barrier, inc=1, device_id=peer, device_id_type=MESH)
    pl.semaphore_wait(barrier, len(peers))


def edge_copies(dp, seq, packed, cot_hbm, words, halo, ws, wr, hs, hr):
    out = []
    for d in range(1, SEQ):
        out.append(send(packed, words.at[seq], ws.at[d - 1], wr.at[d - 1], (dp, (seq + d) % SEQ)))
    out.append(send(cot_hbm.at[:, ROWS - 128 : ROWS], halo.at[0], hs.at[0], hr.at[0], (dp, (seq + 1) % SEQ)))
    out.append(send(cot_hbm.at[:, 0:128], halo.at[1], hs.at[1], hr.at[1], (dp, (seq + SEQ - 1) % SEQ)))
    return out


def pack_part(p, me, unit_s, own, oth):
    core = me[3]

    def piece(j, _):
        at = [None] * 3
        at[ORDER[p][0]], at[ORDER[p][1]], at[ORDER[p][2]] = j // 16, (j // 4) % 4, j % 4
        x, y, z = at
        unit = (y // 2) * 8 + z * 2
        rows = pl.ds(pl.multiple_of(p * 256 + x * 64 + (y % 2) * 32, 32), 32)
        own[p, j] = unit_s[unit + core, rows, :].astype(BF16)
        oth[p, j] = unit_s[unit + 1 - core, rows, :].astype(BF16)
        return 0

    lax.fori_loop(0, 64, piece, 0)


def pair_copy(p, me, oth, recv_d, ss, rs):
    x, y, z, core = me
    return send(oth.at[p], recv_d.at[p], ss.at[p], rs.at[p], device_at(x, y, z, 1 - core))


def pair_sum(p, own, recv_d):
    def piece(j, _):
        own[p, j] = (own[p, j].astype(F32) + recv_d[p, j].astype(F32)).astype(BF16)
        return 0

    lax.fori_loop(0, 64, piece, 0)


def ring_copies(p, me, own, recv_1, ss, rs):
    axis = ORDER[p][0]
    out = []
    for d in range(1, 4):
        to = list(me)
        to[axis] = (me[axis] + d) % 4
        src = own.at[p, pl.ds(to[axis] * 16, 16)]
        out.append(send(src, recv_1.at[p, d - 1], ss.at[p, d - 1], rs.at[p, d - 1], device_at(*to)))
    return out


def ring_sum(p, me, own, recv_1, buf_2):
    base = me[ORDER[p][0]] * 16

    def piece(j, _):
        total = own[p, base + j].astype(F32)
        for d in range(3):
            total = total + recv_1[p, d, j].astype(F32)
        buf_2[p, j] = total.astype(BF16)
        return 0

    lax.fori_loop(0, 16, piece, 0)


def plane_copies(p, me, buf_2, recv_2, ss, rs):
    b, c = ORDER[p][1], ORDER[p][2]
    out = []
    for e in range(1, 16):
        to = list(me)
        to[b] = (me[b] + e // 4) % 4
        to[c] = (me[c] + e % 4) % 4
        src = buf_2.at[p, to[b] * 4 + to[c]]
        out.append(send(src, recv_2.at[p, e - 1], ss.at[p, e - 1], rs.at[p, e - 1], device_at(*to)))
    return out


def plane_sum(p, me, buf_2, recv_2, fin):
    total = buf_2[p, me[ORDER[p][1]] * 4 + me[ORDER[p][2]]].astype(F32)
    for e in range(15):
        total = total + recv_2[p, e].astype(F32)
    fin[p] = total.astype(BF16)


def share_copies(dp, seq, fin, gath, ss, rs):
    return [
        send(fin, gath.at[seq], ss.at[d - 1], rs.at[d - 1], (dp, (seq + d) % SEQ)) for d in range(1, SEQ)
    ]


def place_tower(gath, flat, tower_ref):
    for s in range(SEQ):
        for p in range(3):
            r0 = p * 256 + (s % 4) * 64 + (s // 4) * 32
            flat[r0 : r0 + 32, :] = gath[s, p].astype(F32)
    for t in range(K2):
        for ct in range(4):
            j = 4 * t + ct
            tower_ref[t, :, ct * 128 : (ct + 1) * 128] = flat[38 * j : 38 * j + 38, :]


def pack_stem(stem_acc, gain_acc, stb):
    even = stem_acc[0:C1, :]
    odd = pltpu.roll(stem_acc[C1:, :], 60, 1) if False else jnp.concatenate(
        [stem_acc[C1:, 4:64], stem_acc[C1:, 0:4]], axis=1
    )
    lane = lax.broadcasted_iota(I32, (C1, 64), 1)
    gain = jnp.sum(gain_acc[...], axis=1, keepdims=True)
    both = jnp.where(lane < 60, even + odd, jnp.where(lane == 60, gain, 0.0)).T
    for i in range(16):
        stb[i] = both[(i % 8) * 8 : (i % 8) * 8 + 8, (i // 8) * 256 : (i // 8) * 256 + 256]


def stem_plane_copies(me, src_of, recv, slot_of, ss, rs):
    x, y, z, core = me
    out = []
    for e in range(1, 16):
        tx, ty = (x + e // 4) % 4, (y + e % 4) % 4
        out.append(
            send(src_of(tx * 4 + ty), recv.at[slot_of(e)], ss.at[e - 1], rs.at[e - 1], device_at(tx, ty, z, core))
        )
    return out


def stem_line_copies(me, piece, recv, ss, rs):
    x, y, z, core = me
    out = []
    for e in range(1, 8):
        to = device_at(x, y, (z + e // 2) % 4, (core + e % 2) % 2)
        out.append(send(piece, recv.at[z * 2 + core], ss.at[e - 1], rs.at[e - 1], to))
    return out


def place_stem(gath, stem_ref, gain_ref):
    for half in range(2):
        cols = slice(half * 256, half * 256 + 256)
        for s in range(K1):
            r = 4 * s
            stem_ref[s, :, cols] = gath[half * 8 + r // 8, r % 8 : r % 8 + 4, :]
        gain_ref[:, cols] = gath[half * 8 + 7, 4:5, :]


def start(copies):
    for c in copies:
        c.start()


def wait(copies):
    for c in copies:
        c.wait()


def whole_kernel(
    packed, rc_ref, sh_ref, cot_hbm, sw_ref, gain, w_hbm,
    resp_hbm, stem_ref, gain_ref, tower_ref,
    cot_v, w5, sw_f, wcat, gain_b, wt, gt, oh, act, xt,
    stem_s, ag_s, sg_s, gain_acc, stem_acc, resp_v, tg_s, unit_s,
    words, halo, own, oth, recv_d, recv_1, buf_2, recv_2, fin, gath, flat,
    stb, recv_a, piece_a, recv_b, piece_b, gath_a,
    sems, ws, wr, hs, hr, ds, dr, s1, r1, s2, r2, s3, r3, sa, ra, sb, rb, sg, rg,
):
    dp, seq = lax.axis_index("dp"), lax.axis_index("seq")
    x, y, z, core = seq % 4, (dp // 8) * 2 + seq // 4, (dp // 2) % 4, dp % 2
    me = (x, y, z, core)
    c1 = pltpu.make_async_copy(cot_hbm, cot_v, sems.at[0])
    c2 = pltpu.make_async_copy(w_hbm, w5, sems.at[1])
    c1.start()
    c2.start()
    greet(me)
    edges = edge_copies(dp, seq, packed, cot_hbm, words, halo, ws, wr, hs, hr)
    start(edges)
    words[seq] = packed[...]
    prep_stem_weight(sw_ref, sw_f, wcat, gain, gain_b)
    c2.wait()
    prep_tower_weight(w5, wt)
    wait(edges)
    decode(words, rc_ref[0], sh_ref[0], seq, oh)
    c1.wait()
    prep_cot(cot_v, halo, seq, gt)
    main_loop(oh, wcat, gain_b, seq, gt, wt, stem_s, ag_s, sg_s, act, gain_acc, stem_acc)
    pack_stem(stem_acc, gain_acc, stb)
    level_a = stem_plane_copies(me, lambda a: stb.at[a], recv_a, lambda e: e - 1, sa, ra)
    start(level_a)
    shift_act(act, xt)
    tower_part(cot_v, xt, tg_s, unit_s)
    pairs = []
    for p in range(3):
        pack_part(p, me, unit_s, own, oth)
        pairs.append(pair_copy(p, me, oth, recv_d, ds, dr))
        pairs[p].start()

    def resp(lo, hi):
        def group(g, _):
            response_step(xt, w5, resp_v, pl.multiple_of(g * CH, CH), CH)
            return 0

        lax.fori_loop(lo, hi, group, 0)

    resp(0, 2)
    rings = []
    for p in range(3):
        pairs[p].wait()
        pair_sum(p, own, recv_d)
        rings.append(ring_copies(p, me, own, recv_1, s1, r1))
        start(rings[p])
    wait(level_a)
    total = stb[x * 4 + y]
    for e in range(15):
        total = total + recv_a[e]
    piece_a[...] = total
    recv_b[z * 2 + core] = total
    level_b = stem_line_copies(me, piece_a, recv_b, sb, rb)
    start(level_b)
    resp(2, 5)
    planes = []
    wait(level_b)
    total = recv_b[0]
    for e in range(1, 8):
        total = total + recv_b[e]
    piece_b[...] = total
    gath_a[x * 4 + y] = total
    level_c = stem_plane_copies(me, lambda a: piece_b, gath_a, lambda e: x * 4 + y, sg, rg)
    start(level_c)
    resp(5, 7)
    response_step(xt, w5, resp_v, 7 * CH, 128)
    c3 = pltpu.make_async_copy(resp_v, resp_hbm, sems.at[0])
    c3.start()
    for p in range(3):
        wait(rings[p])
        ring_sum(p, me, own, recv_1, buf_2)
        planes.append(plane_copies(p, me, buf_2, recv_2, s2, r2))
        start(planes[p])
    wait(level_c)
    place_stem(gath_a, stem_ref, gain_ref)
    for p in range(3):
        wait(planes[p])
        plane_sum(p, me, buf_2, recv_2, fin)
    share = share_copies(dp, seq, fin, gath, s3, r3)
    start(share)
    gath[seq] = fin[...]
    c3.wait()
    wait(share)
    place_tower(gath, flat, tower_ref)


def scratch():
    V = pltpu.VMEM
    D = pltpu.SemaphoreType.DMA
    return [
        V((F2, ROWS), BF16),
        V((K2, F2, C1), BF16),
        V((64, 2 * C1), F32),
        V((2 * C1, 64), BF16),
        V((C1, 128), F32),
        V((C1, KF), BF16),
        V((KF, ROWS), BF16),
        V((64, WIDE), BF16),
        V((C1, WIDE), BF16),
        V((K2 * C1, ROWS), BF16),
        V((2 * C1, CH), F32),
        V((C1, CH), F32),
        V((2 * C1, CH), BF16),
        V((C1, 128), F32),
        V((2 * C1, 64), F32),
        V((F2, ROWS), BF16),
        V((F2, C1), F32),
        V((16, UNIT, 128), F32),
        V((SEQ, 1, 256), I32),
        V((2, F2, 128), BF16),
        V((3, 64, 32, 128), BF16),
        V((3, 64, 32, 128), BF16),
        V((3, 64, 32, 128), BF16),
        V((3, 3, 16, 32, 128), BF16),
        V((3, 16, 32, 128), BF16),
        V((3, 15, 32, 128), BF16),
        V((3, 32, 128), BF16),
        V((SEQ, 3, 32, 128), BF16),
        V((UNIT, 128), F32),
        V((16, 8, 256), F32),
        V((15, 8, 256), F32),
        V((8, 256), F32),
        V((8, 8, 256), F32),
        V((8, 256), F32),
        V((16, 8, 256), F32),
        D((2,)), D((7,)), D((7,)), D((2,)), D((2,)), D((3,)), D((3,)),
        D((3, 3)), D((3, 3)), D((3, 15)), D((3, 15)), D((7,)), D((7,)),
        D((15,)), D((15,)), D((7,)), D((7,)), D((15,)), D((15,)),
    ]


def shards(packed, rc_flags, shifts, cotangent, stem_weight, pool_gain, tower_weight):
    S = pl.BlockSpec(memory_space=pltpu.SMEM)
    VM = pl.BlockSpec(memory_space=pltpu.VMEM)
    A = pl.BlockSpec(memory_space=pl.ANY)
    resp, stem, gain, tower = pl.pallas_call(
        whole_kernel,
        out_shape=(
            jax.ShapeDtypeStruct((F2, ROWS), BF16),
            jax.ShapeDtypeStruct((K1, 4, C1), F32),
            jax.ShapeDtypeStruct((1, C1), F32),
            jax.ShapeDtypeStruct((K2, 38, C1), F32),
        ),
        in_specs=[VM, S, S, A, VM, VM, A],
        out_specs=(A, VM, VM, VM),
        scratch_shapes=scratch(),
        compiler_params=pltpu.CompilerParams(
            vmem_limit_bytes=62 * 1024 * 1024, collective_id=0, has_side_effects=True
        ),
    )(
        packed, rc_flags, shifts, cotangent[0].T, stem_weight, pool_gain[None],
        jnp.transpose(tower_weight, (1, 0, 2)),
    )
    return resp.T[None], stem, gain[0], jnp.transpose(tower, (1, 0, 2))


def solution(mesh):
    in_specs = (P("dp", "seq"), P("dp"), P("dp"), P("dp", "seq", None), P(), P(), P())
    out_specs = (P("dp", "seq", None), P(), P(), P("dp", None, None))
    return jax.shard_map(shards, mesh=mesh, in_specs=in_specs, out_specs=out_specs, check_vma=False)
```

```python
import functools
import jax
import jax.numpy as jnp
from jax import lax
from jax.experimental import pallas as pl
from jax.experimental.pallas import tpu as pltpu
from jax.sharding import PartitionSpec as P

F32, BF16, I32 = jnp.float32, jnp.bfloat16, jnp.int32
C1, F2, K1, K2 = 512, 608, 15, 5
ROWS = 1920
WIDE = 2048
KF = 3072
UNIT = 768
SEQ = 8
CH = 256


def dot(a, b):
    return lax.dot_general(a, b, (((1,), (0,)), ((), ())), preferred_element_type=F32)


def dot_nt(a, b):
    return lax.dot_general(a, b, (((1,), (1,)), ((), ())), preferred_element_type=F32)


def prep_stem_weight(sw_ref, sw_f, wcat, gain, gain_b):
    sw_f[60:68, :] = jnp.zeros((8, C1), F32)
    for s in range(K1):
        v = sw_ref[s].astype(F32) * 0.25
        sw_f[4 * s : 4 * s + 4, :] = v
        sw_f[68 + 4 * s : 72 + 4 * s, :] = v
    w = sw_f[...].T
    lane = lax.broadcasted_iota(I32, (C1, 128), 1)
    wcat[0:C1, :] = jnp.where(lane < 64, w, -w).astype(BF16)
    wcat[C1:, :] = w.astype(BF16)
    gain_b[...] = jnp.broadcast_to(gain[...], (128, C1)).T * 2.0


def prep_tower_weight(w5, wt):
    flat = w5.reshape(K2 * F2, C1)

    def block(i, _):
        r0 = pl.multiple_of(i * 128, 128)
        wt[:, pl.ds(r0, 128)] = flat[pl.ds(r0, 128), :].T
        return 0

    lax.fori_loop(0, (K2 * F2) // 128, block, 0, unroll=True)
    tail = K2 * F2 - (K2 * F2) // 128 * 128
    v = jnp.concatenate([flat[K2 * F2 - tail :, :], jnp.zeros((128 - tail, C1), BF16)], axis=0)
    wt[:, KF - 128 :] = v.T


def prep_cot(cot_v, gt):
    def rows(i, _):
        r0 = pl.multiple_of(i * 16, 16)
        full = cot_v[pl.ds(r0, 16), :]
        for t in range(K2):
            s = 2 - t
            v = full if s == 0 else pltpu.roll(full, (-s) % ROWS, 1)
            gt[pl.ds(pl.multiple_of(t * F2 + r0, 16), 16), :] = v
        return 0

    lax.fori_loop(0, F2 // 16, rows, 0, unroll=True)
    gt[K2 * F2 : KF, :] = jnp.zeros((KF - K2 * F2, ROWS), BF16)


def rim_cot(cot_v, halo, seq, gt):
    lane = lax.broadcasted_iota(I32, (16, 128), 1)
    for r in range(0, F2, 16):
        rs = slice(r, r + 16)
        nxt = jnp.where(seq < SEQ - 1, halo[1, rs, :].astype(F32), 0.0)
        prv = jnp.where(seq > 0, halo[0, rs, :].astype(F32), 0.0)
        rim = jnp.where(lane < 64, nxt, prv).astype(BF16)
        ring = jnp.concatenate([cot_v[rs, ROWS - 256 : ROWS], rim, cot_v[rs, 0:256]], axis=1)
        for t in range(K2):
            s = 2 - t
            if s != 0:
                v = pltpu.roll(ring, (-s) % 640, 1)
                gt[t * F2 + r : t * F2 + r + 16, ROWS - 128 : ROWS] = v[:, 128:256]
                gt[t * F2 + r : t * F2 + r + 16, 0:128] = v[:, 384:512]


def decode(words, rc, shift, seq, oh):
    take = jnp.where(rc == 1, SEQ - 1 - seq, seq)
    slot = lax.broadcasted_iota(I32, (SEQ, 1, CH), 0)
    w8 = words[...]
    own = jnp.sum(jnp.where(slot == take, w8, 0), axis=0)
    low = jnp.sum(jnp.where(slot == take - 1, w8, 0), axis=0)
    high = jnp.sum(jnp.where(slot == take + 1, w8, 0), axis=0)
    lane = lax.broadcasted_iota(I32, (1, 128), 1)
    rim = jnp.where(lane == 127, low[:, 128:256], jnp.where(lane == 0, high[:, 0:128], 0))
    row = jnp.broadcast_to(jnp.concatenate([own, rim], axis=1), (8, 384))
    after = jnp.where(rc == 1, pltpu.roll(row, 1, 1), pltpu.roll(row, 383, 1))
    sub = lax.broadcasted_iota(I32, (8, 384), 0)
    planes = (jnp.where(sub < 4, row, after) >> (8 * (sub & 3))) & 255
    planes = planes.astype(F32).astype(BF16)
    src = lax.broadcasted_iota(I32, (384, CH), 0)
    src = jnp.where(src == 383, -1, src)
    part = lax.broadcasted_iota(I32, (64, CH), 0)
    s = part >> 2
    want = jnp.where(rc == 1, 3 - (part & 3), part & 3)

    def chunk(i, _):
        u0 = pl.multiple_of(i * CH, CH)
        u = u0 + lax.broadcasted_iota(I32, (1, CH), 1)
        q = jnp.where(u < 1984, u, u - WIDE)
        b0 = 2 * q - 7 - shift
        j0 = (((b0 + 30) * 34953) >> 19) - 2
        i0 = b0 - 15 * j0
        at = jnp.where(rc == 1, 255 - j0, j0)
        sel = jnp.where(src == at, 1.0, 0.0).astype(BF16)
        got = dot(planes, sel).astype(I32)
        word_a = got[0:1] + (got[1:2] << 8) + (got[2:3] << 16) + (got[3:4] << 24)
        word_b = got[4:5] + (got[5:6] << 8) + (got[6:7] << 16) + (got[7:8] << 24)
        d = i0 + s
        late = d >= 15
        word = jnp.where(late, word_b, word_a)
        d = jnp.where(late, d - 15, d)
        d = jnp.where(rc == 1, 14 - d, d)
        where = 2 * ROWS * seq + b0 + s
        good = (where >= 0) & (where < 2 * ROWS * SEQ)
        hit = (((word >> (2 * d)) & 3) == want) & good
        hot = jnp.where(hit, 1.0, 0.0).astype(BF16)
        oh[0:64, pl.ds(u0, CH)] = hot
        oh[64:128, pl.ds(u0, CH)] = hot
        return 0

    lax.fori_loop(0, WIDE // CH, chunk, 0, unroll=True)


GELU_A = 0.7978845608028654
GELU_B = 0.044715


def pool(hd, mean, gain2):
    gd = gain2 * hd
    t = jnp.tanh(gd)
    hx = mean + t * hd
    h2 = hx * hx
    th = jnp.tanh(hx * (2 * GELU_A + (8 * GELU_A * GELU_B) * h2))
    p1 = 1.0 + th
    act = hx * p1
    dgelu = p1 * (0.25 + hx * (2.0 - p1) * (0.5 * GELU_A + (6 * GELU_A * GELU_B) * h2))
    k = gd * (1.0 - t * t)
    m1 = (1.0 + t) + k
    return act, dgelu * m1, dgelu * (2.0 - m1), dgelu * (hd * k)


def span(n):
    return slice(n * CH, min((n + 1) * CH, ROWS))


def ag_chunk(n, wt, gt, ag):
    ag[:, span(n)] = dot(wt[...], gt[:, span(n)]).astype(BF16)


def stem_chunk(n, wcat, oh, stem_s):
    stem_s[n % 2] = dot(wcat[...], oh[:, n * CH : (n + 1) * CH])


def pool_chunk(n, seq, stem_s, gain_b, act, fac):
    for r in range(0, C1, 16):
        for lt in range(2):
            cols = slice(lt * 128, lt * 128 + 128)
            at = slice(n * CH + lt * 128, n * CH + lt * 128 + 128)
            a, f1, f2, f3 = pool(
                stem_s[n % 2, r : r + 16, cols], stem_s[n % 2, C1 + r : C1 + r + 16, cols], gain_b[r : r + 16, :]
            )
            if at.start >= ROWS:
                lane = lax.broadcasted_iota(I32, (16, 128), 1)
                out = ((lane < 64) & (seq == SEQ - 1)) | ((lane >= 64) & (seq == 0))
                a = jnp.where(out, 0.0, a)
            else:
                fac[0, r : r + 16, at] = f1.astype(BF16)
                fac[1, r : r + 16, at] = f2.astype(BF16)
                fac[2, r : r + 16, at] = f3.astype(BF16)
            act[r : r + 16, at] = a.astype(BF16)


def back_chunk(n, ag, fac, sg_s, gain_acc):
    for r in range(0, C1, 16):
        for c0 in range(span(n).start, span(n).stop, 128):
            rs, cs = slice(r, r + 16), slice(c0, c0 + 128)
            o = slice(c0 % CH, c0 % CH + 128)
            g = ag[rs, cs]
            sg_s[n % 2, rs, o] = g * fac[0, rs, cs]
            sg_s[n % 2, C1 + r : C1 + r + 16, o] = g * fac[1, rs, cs]
            gain_acc[rs, :] += g.astype(F32) * fac[2, rs, cs].astype(F32)


def stem_grad_chunk(n, sg_s, oh, stem_acc):
    w = span(n).stop - span(n).start
    stem_acc[...] += dot_nt(sg_s[n % 2, :, 0:w], oh[0:64, span(n)])


def shift_act(t, act, xt):
    s = t - 2
    for r in range(0, C1, 16):
        v = pltpu.roll(act[r : r + 16, :], (-s) % WIDE, 1)
        xt[t - t // 3, r : r + 16, :] = v[:, 0:ROWS]


TAPS = (2, 1, 3, 0, 4)


def tower_tap(i, cot_v, act, xt, tg_s, unit_s):
    t = TAPS[i]
    rhs = act[:, 0:ROWS] if t == 2 else xt[t - t // 3]
    tg_s[i % 2] = dot_nt(cot_v[...], rhs)
    for d in range(16):
        for ct in range(4):
            piece = tg_s[i % 2, 38 * d : 38 * d + 38, ct * 128 : (ct + 1) * 128]
            unit_s[d, 152 * i + 38 * ct : 152 * i + 38 * ct + 38, :] = piece


def resp_chunk(n, w5, act, xt, resp_v):
    cols = span(n)
    taps = jnp.concatenate([w5[t] for t in range(K2)], axis=1)
    rhs = jnp.concatenate([act[:, cols] if t == 2 else xt[t - t // 3, :, cols] for t in range(K2)], axis=0)
    resp_v[:, cols] = dot(taps, rhs).astype(BF16)


ORDER = ((0, 1, 2), (1, 2, 0), (2, 0, 1))
MESH = pl.DeviceIdType.MESH


def device_at(x, y, z, core):
    return ((y // 2) * 8 + z * 2 + core, (y % 2) * 4 + x)


def send(src, dst, ssem, rsem, to):
    return pltpu.make_async_remote_copy(
        src_ref=src, dst_ref=dst, send_sem=ssem, recv_sem=rsem, device_id=to, device_id_type=MESH
    )


def greet(me):
    barrier = pltpu.get_barrier_semaphore()
    x, y, z, core = me
    peers = []
    for dx in range(4):
        for dy in range(4):
            for dz in range(4):
                if (dx, dy, dz) != (0, 0, 0) and 0 in (dx, dy, dz):
                    peers.append(device_at((x + dx) % 4, (y + dy) % 4, (z + dz) % 4, core))
    for dz in range(4):
        peers.append(device_at(x, y, (z + dz) % 4, 1 - core))
    for peer in peers:
        pl.semaphore_signal(barrier, inc=1, device_id=peer, device_id_type=MESH)
    pl.semaphore_wait(barrier, len(peers))


def edge_copies(dp, seq, packed, cot_hbm, words, halo, ws, wr, hs, hr):
    out = []
    for d in range(1, SEQ):
        out.append(send(packed, words.at[seq], ws.at[d - 1], wr.at[d - 1], (dp, (seq + d) % SEQ)))
    out.append(send(cot_hbm.at[:, ROWS - 128 : ROWS], halo.at[0], hs.at[0], hr.at[0], (dp, (seq + 1) % SEQ)))
    out.append(send(cot_hbm.at[:, 0:128], halo.at[1], hs.at[1], hr.at[1], (dp, (seq + SEQ - 1) % SEQ)))
    return out


def pack_part(p, me, unit_s, own, oth):
    core = me[3]

    def piece(j, _):
        at = [None] * 3
        at[ORDER[p][0]], at[ORDER[p][1]], at[ORDER[p][2]] = j // 16, (j // 4) % 4, j % 4
        x, y, z = at
        unit = (y // 2) * 8 + z * 2
        rows = pl.ds(pl.multiple_of(p * 256 + x * 64 + (y % 2) * 32, 32), 32)
        own[p, j] = unit_s[unit + core, rows, :].astype(BF16)
        oth[p, j] = unit_s[unit + 1 - core, rows, :].astype(BF16)
        return 0

    lax.fori_loop(0, 64, piece, 0)


def pair_copy(p, me, oth, recv_d, ss, rs):
    x, y, z, core = me
    return send(oth.at[p], recv_d.at[p], ss.at[p], rs.at[p], device_at(x, y, z, 1 - core))


def pair_sum(p, own, recv_d):
    def piece(j, _):
        own[p, j] = (own[p, j].astype(F32) + recv_d[p, j].astype(F32)).astype(BF16)
        return 0

    lax.fori_loop(0, 64, piece, 0)


def ring_copies(p, me, own, recv_1, ss, rs):
    axis = ORDER[p][0]
    out = []
    for d in range(1, 4):
        to = list(me)
        to[axis] = (me[axis] + d) % 4
        src = own.at[p, pl.ds(to[axis] * 16, 16)]
        out.append(send(src, recv_1.at[p, d - 1], ss.at[p, d - 1], rs.at[p, d - 1], device_at(*to)))
    return out


def ring_sum(p, me, own, recv_1, buf_2):
    base = me[ORDER[p][0]] * 16

    def piece(j, _):
        total = own[p, base + j].astype(F32)
        for d in range(3):
            total = total + recv_1[p, d, j].astype(F32)
        buf_2[p, j] = total.astype(BF16)
        return 0

    lax.fori_loop(0, 16, piece, 0)


def plane_copies(p, me, buf_2, recv_2, ss, rs):
    b, c = ORDER[p][1], ORDER[p][2]
    out = []
    for e in range(1, 16):
        to = list(me)
        to[b] = (me[b] + e // 4) % 4
        to[c] = (me[c] + e % 4) % 4
        src = buf_2.at[p, to[b] * 4 + to[c]]
        out.append(send(src, recv_2.at[p, e - 1], ss.at[p, e - 1], rs.at[p, e - 1], device_at(*to)))
    return out


def plane_sum(p, me, buf_2, recv_2, fin):
    total = buf_2[p, me[ORDER[p][1]] * 4 + me[ORDER[p][2]]].astype(F32)
    for e in range(15):
        total = total + recv_2[p, e].astype(F32)
    fin[p] = total.astype(BF16)


def share_copies(dp, seq, fin, gath, ss, rs):
    return [
        send(fin, gath.at[seq], ss.at[d - 1], rs.at[d - 1], (dp, (seq + d) % SEQ)) for d in range(1, SEQ)
    ]


def place_tower(gath, flat, tower_ref):
    for s in range(SEQ):
        for p in range(3):
            r0 = p * 256 + (s % 4) * 64 + (s // 4) * 32
            flat[r0 : r0 + 32, :] = gath[s, p].astype(F32)
    for i, t in enumerate(TAPS):
        for ct in range(4):
            j = 4 * i + ct
            tower_ref[t, :, ct * 128 : (ct + 1) * 128] = flat[38 * j : 38 * j + 38, :]


def pack_stem(stem_acc, gain_acc, gain, stb):
    even = stem_acc[0:C1, :]
    odd = jnp.concatenate([stem_acc[C1:, 4:64], stem_acc[C1:, 0:4]], axis=1)
    lane = lax.broadcasted_iota(I32, (C1, 64), 1)
    total = jnp.sum(gain_acc[...], axis=1, keepdims=True)
    both = jnp.where(lane < 60, even + odd, jnp.where(lane == 60, total, 0.0)).T
    row = lax.broadcasted_iota(I32, (8, 1), 0)
    last = jnp.where(row == 4, both[56:64] * (4.0 / gain[...]), both[56:64])
    for i in range(16):
        cols = slice((i // 8) * 256, (i // 8) * 256 + 256)
        stb[i] = last[:, cols] if i % 8 == 7 else both[(i % 8) * 8 : (i % 8) * 8 + 8, cols]


def stem_plane_copies(me, src_of, recv, slot_of, ss, rs):
    x, y, z, core = me
    out = []
    for e in range(1, 16):
        tx, ty = (x + e // 4) % 4, (y + e % 4) % 4
        out.append(
            send(src_of(tx * 4 + ty), recv.at[slot_of(e)], ss.at[e - 1], rs.at[e - 1], device_at(tx, ty, z, core))
        )
    return out


def stem_line_copies(me, piece, recv, ss, rs):
    x, y, z, core = me
    out = []
    for e in range(1, 8):
        to = device_at(x, y, (z + e // 2) % 4, (core + e % 2) % 2)
        out.append(send(piece, recv.at[z * 2 + core], ss.at[e - 1], rs.at[e - 1], to))
    return out


def place_stem(gath, stem_ref, gain_ref):
    for half in range(2):
        cols = slice(half * 256, half * 256 + 256)
        for s in range(K1):
            r = 4 * s
            stem_ref[s, :, cols] = gath[half * 8 + r // 8, r % 8 : r % 8 + 4, :]
        gain_ref[:, cols] = gath[half * 8 + 7, 4:5, :]


def start(copies):
    for c in copies:
        c.start()


def wait(copies):
    for c in copies:
        c.wait()


def whole_kernel(
    packed, rc_ref, sh_ref, cot_hbm, sw_ref, gain, w_hbm,
    resp_hbm, stem_ref, gain_ref, tower_ref,
    cot_v, w5, sw_f, wcat, gain_b, wt, gt, oh, act, xt,
    stem_s, ag, fac, sg_s, gain_acc, stem_acc, tg_s, unit_s,
    words, halo, own, oth, recv_d, recv_1, buf_2, recv_2, fin, gath, flat,
    stb, recv_a, piece_a, recv_b, piece_b, gath_a,
    sems, ws, wr, hs, hr, ds, dr, s1, r1, s2, r2, s3, r3, sa, ra, sb, rb, sg, rg,
):
    dp, seq = lax.axis_index("dp"), lax.axis_index("seq")
    x, y, z, core = seq % 4, (dp // 8) * 2 + seq // 4, (dp // 2) % 4, dp % 2
    me = (x, y, z, core)
    c1 = pltpu.make_async_copy(cot_hbm, cot_v, sems.at[0])
    c2 = pltpu.make_async_copy(w_hbm, w5, sems.at[1])
    c1.start()
    c2.start()
    greet(me)
    edges = edge_copies(dp, seq, packed, cot_hbm, words, halo, ws, wr, hs, hr)
    start(edges)
    words[seq] = packed[...]
    gain_acc[...] = jnp.zeros_like(gain_acc)
    stem_acc[...] = jnp.zeros_like(stem_acc)
    unit_s[:, 760:768, :] = jnp.zeros((16, 8, 128), F32)
    prep_stem_weight(sw_ref, sw_f, wcat, gain, gain_b)
    c1.wait()
    prep_cot(cot_v, gt)
    c2.wait()
    prep_tower_weight(w5, wt)
    ag_chunk(1, wt, gt, ag)
    wait(edges)
    decode(words, rc_ref[0], sh_ref[0], seq, oh)
    rim_cot(cot_v, halo, seq, gt)
    for n in range(8):
        stem_chunk(n, wcat, oh, stem_s)
        if n < 5:
            ag_chunk(n + 2, wt, gt, ag)
        pool_chunk(n, seq, stem_s, gain_b, act, fac)

    def tap(i):
        if i != 0:
            shift_act(TAPS[i], act, xt)
        tower_tap(i, cot_v, act, xt, tg_s, unit_s)

    pairs, rings, planes = [], [], []

    def pair(p):
        pack_part(p, me, unit_s, own, oth)
        pairs.append(pair_copy(p, me, oth, recv_d, ds, dr))
        pairs[p].start()

    def ring(p):
        pairs[p].wait()
        pair_sum(p, own, recv_d)
        rings.append(ring_copies(p, me, own, recv_1, s1, r1))
        start(rings[p])

    def plane(p):
        wait(rings[p])
        ring_sum(p, me, own, recv_1, buf_2)
        planes.append(plane_copies(p, me, buf_2, recv_2, s2, r2))
        start(planes[p])

    def resp(n):
        resp_chunk(n, w5, act, xt, cot_v)

    tap(0)
    tap(1)
    pair(0)
    tap(2)
    ring(0)
    tap(3)
    pair(1)
    tap(4)
    pair(2)
    ring(1)
    ag_chunk(0, wt, gt, ag)
    ag_chunk(7, wt, gt, ag)
    ring(2)
    for n in range(8):
        back_chunk(n, ag, fac, sg_s, gain_acc)
        stem_grad_chunk(n, sg_s, oh, stem_acc)
    pack_stem(stem_acc, gain_acc, gain, stb)
    level_a = stem_plane_copies(me, lambda a: stb.at[a], recv_a, lambda e: e - 1, sa, ra)
    start(level_a)
    resp(0)
    resp(1)
    plane(0)
    resp(2)
    resp(3)
    wait(level_a)
    total = stb[x * 4 + y]
    for e in range(15):
        total = total + recv_a[e]
    piece_a[...] = total
    recv_b[z * 2 + core] = total
    level_b = stem_line_copies(me, piece_a, recv_b, sb, rb)
    start(level_b)
    plane(1)
    resp(4)
    resp(5)
    wait(level_b)
    total = recv_b[0]
    for e in range(1, 8):
        total = total + recv_b[e]
    piece_b[...] = total
    gath_a[x * 4 + y] = total
    level_c = stem_plane_copies(me, lambda a: piece_b, gath_a, lambda e: x * 4 + y, sg, rg)
    start(level_c)
    plane(2)
    resp(6)
    resp(7)
    c3 = pltpu.make_async_copy(cot_v, resp_hbm, sems.at[0])
    c3.start()
    wait(level_c)
    place_stem(gath_a, stem_ref, gain_ref)
    for p in range(3):
        wait(planes[p])
        plane_sum(p, me, buf_2, recv_2, fin)
    share = share_copies(dp, seq, fin, gath, s3, r3)
    start(share)
    gath[seq] = fin[...]
    c3.wait()
    wait(share)
    place_tower(gath, flat, tower_ref)


def scratch():
    V = pltpu.VMEM
    D = pltpu.SemaphoreType.DMA
    return [
        V((F2, ROWS), BF16),
        V((K2, F2, C1), BF16),
        V((128, C1), F32),
        V((2 * C1, 128), BF16),
        V((C1, 128), F32),
        V((C1, KF), BF16),
        V((KF, ROWS), BF16),
        V((128, WIDE), BF16),
        V((C1, WIDE), BF16),
        V((K2 - 1, C1, ROWS), BF16),
        V((2, 2 * C1, CH), F32),
        V((C1, ROWS), BF16),
        V((3, C1, ROWS), BF16),
        V((2, 2 * C1, CH), BF16),
        V((C1, 128), F32),
        V((2 * C1, 64), F32),
        V((2, F2, C1), F32),
        V((16, UNIT, 128), F32),
        V((SEQ, 1, 256), I32),
        V((2, F2, 128), BF16),
        V((3, 64, 32, 128), BF16),
        V((3, 64, 32, 128), BF16),
        V((3, 64, 32, 128), BF16),
        V((3, 3, 16, 32, 128), BF16),
        V((3, 16, 32, 128), BF16),
        V((3, 15, 32, 128), BF16),
        V((3, 32, 128), BF16),
        V((SEQ, 3, 32, 128), BF16),
        V((UNIT, 128), F32),
        V((16, 8, 256), F32),
        V((15, 8, 256), F32),
        V((8, 256), F32),
        V((8, 8, 256), F32),
        V((8, 256), F32),
        V((16, 8, 256), F32),
        D((2,)), D((7,)), D((7,)), D((2,)), D((2,)), D((3,)), D((3,)),
        D((3, 3)), D((3, 3)), D((3, 15)), D((3, 15)), D((7,)), D((7,)),
        D((15,)), D((15,)), D((7,)), D((7,)), D((15,)), D((15,)),
    ]


def shards(packed, rc_flags, shifts, cotangent, stem_weight, pool_gain, tower_weight):
    S = pl.BlockSpec(memory_space=pltpu.SMEM)
    VM = pl.BlockSpec(memory_space=pltpu.VMEM)
    A = pl.BlockSpec(memory_space=pl.ANY)
    resp, stem, gain, tower = pl.pallas_call(
        whole_kernel,
        out_shape=(
            jax.ShapeDtypeStruct((F2, ROWS), BF16),
            jax.ShapeDtypeStruct((K1, 4, C1), F32),
            jax.ShapeDtypeStruct((1, C1), F32),
            jax.ShapeDtypeStruct((K2, 38, C1), F32),
        ),
        in_specs=[VM, S, S, A, VM, VM, A],
        out_specs=(A, VM, VM, VM),
        scratch_shapes=scratch(),
        compiler_params=pltpu.CompilerParams(
            vmem_limit_bytes=62 * 1024 * 1024, collective_id=0, has_side_effects=True
        ),
    )(
        packed, rc_flags, shifts, cotangent[0].T, stem_weight, pool_gain[None],
        jnp.transpose(tower_weight, (1, 0, 2)),
    )
    return resp.T[None], stem, gain[0], jnp.transpose(tower, (1, 0, 2))


def solution(mesh):
    in_specs = (P("dp", "seq"), P("dp"), P("dp"), P("dp", "seq", None), P(), P(), P())
    out_specs = (P("dp", "seq", None), P(), P(), P("dp", None, None))
    return jax.shard_map(shards, mesh=mesh, in_specs=in_specs, out_specs=out_specs, check_vma=False)
```

```python
import functools
import jax
import jax.numpy as jnp
from jax import lax
from jax.experimental import pallas as pl
from jax.experimental.pallas import tpu as pltpu
from jax.sharding import PartitionSpec as P

F32, BF16, I32 = jnp.float32, jnp.bfloat16, jnp.int32
C1, F2, K1, K2 = 512, 608, 15, 5
ROWS = 1920
WIDE = 2048
KF = 3072
UNIT = 768
SEQ = 8
CH = 256


def dot(a, b):
    return lax.dot_general(a, b, (((1,), (0,)), ((), ())), preferred_element_type=F32)


def dot_nt(a, b):
    return lax.dot_general(a, b, (((1,), (1,)), ((), ())), preferred_element_type=F32)


def prep_stem_weight(sw_ref, sw_f, wcat, gain, gain_b):
    sw_f[60:68, :] = jnp.zeros((8, C1), F32)
    for s in range(K1):
        v = sw_ref[s].astype(F32) * 0.25
        sw_f[4 * s : 4 * s + 4, :] = v
        sw_f[68 + 4 * s : 72 + 4 * s, :] = v
    w = sw_f[...].T
    lane = lax.broadcasted_iota(I32, (C1, 128), 1)
    wcat[0:C1, :] = jnp.where(lane < 64, w, -w).astype(BF16)
    wcat[C1:, :] = w.astype(BF16)
    gain_b[...] = jnp.broadcast_to(gain[...], (128, C1)).T * 2.0


def prep_tower_weight(w5, wt):
    flat = w5.reshape(K2 * F2, C1)

    def block(i, _):
        r0 = pl.multiple_of(i * 128, 128)
        wt[:, pl.ds(r0, 128)] = flat[pl.ds(r0, 128), :].T
        return 0

    lax.fori_loop(0, (K2 * F2) // 128, block, 0, unroll=True)
    tail = K2 * F2 - (K2 * F2) // 128 * 128
    v = jnp.concatenate([flat[K2 * F2 - tail :, :], jnp.zeros((128 - tail, C1), BF16)], axis=0)
    wt[:, KF - 128 :] = v.T


def prep_cot(cot_v, gt):
    def rows(i, _):
        r0 = pl.multiple_of(i * 16, 16)
        full = cot_v[pl.ds(r0, 16), :]
        for t in range(K2):
            s = 2 - t
            v = full if s == 0 else pltpu.roll(full, (-s) % ROWS, 1)
            gt[pl.ds(pl.multiple_of(t * F2 + r0, 16), 16), :] = v
        return 0

    lax.fori_loop(0, F2 // 16, rows, 0, unroll=True)
    gt[K2 * F2 : KF, :] = jnp.zeros((KF - K2 * F2, ROWS), BF16)


def rim_cot(cot_v, halo, seq, rim, gt):
    nxt = jnp.where(seq < SEQ - 1, halo[1].astype(F32), 0.0)
    prv = jnp.where(seq > 0, halo[0].astype(F32), 0.0)
    rim[...] = jnp.concatenate([nxt, jnp.zeros((96, F2), F32), prv], axis=0).T.astype(BF16)
    for r in range(0, F2, 16):
        rs = slice(r, r + 16)
        ring = jnp.concatenate([cot_v[rs, ROWS - 256 : ROWS], rim[rs, :], cot_v[rs, 0:256]], axis=1)
        for t in range(K2):
            s = 2 - t
            if s != 0:
                v = pltpu.roll(ring, (-s) % 640, 1)
                gt[t * F2 + r : t * F2 + r + 16, ROWS - 128 : ROWS] = v[:, 128:256]
                gt[t * F2 + r : t * F2 + r + 16, 0:128] = v[:, 384:512]


def decode(words, rc, shift, seq, oh):
    take = jnp.where(rc == 1, SEQ - 1 - seq, seq)
    slot = lax.broadcasted_iota(I32, (SEQ, 1, CH), 0)
    w8 = words[...]
    own = jnp.sum(jnp.where(slot == take, w8, 0), axis=0)
    low = jnp.sum(jnp.where(slot == take - 1, w8, 0), axis=0)
    high = jnp.sum(jnp.where(slot == take + 1, w8, 0), axis=0)
    lane = lax.broadcasted_iota(I32, (1, 128), 1)
    rim = jnp.where(lane == 127, low[:, 128:256], jnp.where(lane == 0, high[:, 0:128], 0))
    row = jnp.broadcast_to(jnp.concatenate([own, rim], axis=1), (8, 384))
    after = jnp.where(rc == 1, pltpu.roll(row, 1, 1), pltpu.roll(row, 383, 1))
    sub = lax.broadcasted_iota(I32, (8, 384), 0)
    planes = (jnp.where(sub < 4, row, after) >> (8 * (sub & 3))) & 255
    planes = planes.astype(F32).astype(BF16)
    src = lax.broadcasted_iota(I32, (384, CH), 0)
    src = jnp.where(src == 383, -1, src)
    part = lax.broadcasted_iota(I32, (64, CH), 0)
    s = part >> 2
    want = jnp.where(rc == 1, 3 - (part & 3), part & 3)

    def chunk(i, _):
        u0 = pl.multiple_of(i * CH, CH)
        u = u0 + lax.broadcasted_iota(I32, (1, CH), 1)
        q = jnp.where(u < 1984, u, u - WIDE)
        b0 = 2 * q - 7 - shift
        j0 = (((b0 + 30) * 34953) >> 19) - 2
        i0 = b0 - 15 * j0
        at = jnp.where(rc == 1, 255 - j0, j0)
        sel = jnp.where(src == at, 1.0, 0.0).astype(BF16)
        got = dot(planes, sel).astype(I32)
        word_a = got[0:1] + (got[1:2] << 8) + (got[2:3] << 16) + (got[3:4] << 24)
        word_b = got[4:5] + (got[5:6] << 8) + (got[6:7] << 16) + (got[7:8] << 24)
        d = i0 + s
        late = d >= 15
        word = jnp.where(late, word_b, word_a)
        d = jnp.where(late, d - 15, d)
        d = jnp.where(rc == 1, 14 - d, d)
        where = 2 * ROWS * seq + b0 + s
        good = (where >= 0) & (where < 2 * ROWS * SEQ)
        hit = (((word >> (2 * d)) & 3) == want) & good
        hot = jnp.where(hit, 1.0, 0.0).astype(BF16)
        oh[0:64, pl.ds(u0, CH)] = hot
        oh[64:128, pl.ds(u0, CH)] = hot
        return 0

    lax.fori_loop(0, WIDE // CH, chunk, 0, unroll=True)


GELU_A = 0.7978845608028654
GELU_B = 0.044715


def pool(hd, mean, gain2):
    gd = gain2 * hd
    t = jnp.tanh(gd)
    hx = mean + t * hd
    h2 = hx * hx
    th = jnp.tanh(hx * (2 * GELU_A + (8 * GELU_A * GELU_B) * h2))
    p1 = 1.0 + th
    act = hx * p1
    dgelu = p1 * (0.25 + hx * (2.0 - p1) * (0.5 * GELU_A + (6 * GELU_A * GELU_B) * h2))
    k = gd * (1.0 - t * t)
    m1 = (1.0 + t) + k
    return act, dgelu * m1, dgelu * (2.0 - m1), dgelu * (hd * k)


def span(n):
    return slice(n * CH, min((n + 1) * CH, ROWS))


def ag_chunk(n, wt, gt, ag):
    ag[:, span(n)] = dot(wt[...], gt[:, span(n)]).astype(BF16)


def stem_chunk(n, wcat, oh, stem_s):
    stem_s[n % 2] = dot(wcat[...], oh[:, n * CH : (n + 1) * CH])


def pool_chunk(n, seq, stem_s, gain_b, act, fac):
    for r in range(0, C1, 16):
        for lt in range(2):
            cols = slice(lt * 128, lt * 128 + 128)
            at = slice(n * CH + lt * 128, n * CH + lt * 128 + 128)
            a, f1, f2, f3 = pool(
                stem_s[n % 2, r : r + 16, cols], stem_s[n % 2, C1 + r : C1 + r + 16, cols], gain_b[r : r + 16, :]
            )
            if at.start >= ROWS:
                lane = lax.broadcasted_iota(I32, (16, 128), 1)
                out = ((lane < 64) & (seq == SEQ - 1)) | ((lane >= 64) & (seq == 0))
                a = jnp.where(out, 0.0, a)
            else:
                fac[0, r : r + 16, at] = f1.astype(BF16)
                fac[1, r : r + 16, at] = f2.astype(BF16)
                fac[2, r : r + 16, at] = f3.astype(BF16)
            act[r : r + 16, at] = a.astype(BF16)


def back_chunk(n, ag, fac, sg_s, gain_acc):
    for r in range(0, C1, 16):
        for c0 in range(span(n).start, span(n).stop, 128):
            rs, cs = slice(r, r + 16), slice(c0, c0 + 128)
            o = slice(c0 % CH, c0 % CH + 128)
            g = ag[rs, cs]
            sg_s[n % 2, rs, o] = g * fac[0, rs, cs]
            sg_s[n % 2, C1 + r : C1 + r + 16, o] = g * fac[1, rs, cs]
            gain_acc[rs, :] += g.astype(F32) * fac[2, rs, cs].astype(F32)


def stem_grad_chunk(n, sg_s, oh, stem_acc):
    w = span(n).stop - span(n).start
    stem_acc[...] += dot_nt(sg_s[n % 2, :, 0:w], oh[0:64, span(n)])


def shift_act(t, act, xt):
    s = t - 2
    for r in range(0, C1, 16):
        v = pltpu.roll(act[r : r + 16, :], (-s) % WIDE, 1)
        xt[t - t // 3, r : r + 16, :] = v[:, 0:ROWS]


TAPS = (2, 1, 3, 0, 4)


def tower_tap(i, cot_v, act, xt, tg_s, unit_s):
    t = TAPS[i]
    rhs = act[:, 0:ROWS] if t == 2 else xt[t - t // 3]
    tg_s[i % 2] = dot_nt(cot_v[...], rhs)
    for d in range(16):
        for ct in range(4):
            piece = tg_s[i % 2, 38 * d : 38 * d + 38, ct * 128 : (ct + 1) * 128]
            unit_s[d, 152 * i + 38 * ct : 152 * i + 38 * ct + 38, :] = piece


def resp_chunk(n, w5, act, xt, resp_v):
    cols = span(n)
    taps = jnp.concatenate([w5[t] for t in range(K2)], axis=1)
    rhs = jnp.concatenate([act[:, cols] if t == 2 else xt[t - t // 3, :, cols] for t in range(K2)], axis=0)
    resp_v[:, cols] = dot(taps, rhs).astype(BF16)


ORDER = ((0, 1, 2), (1, 2, 0), (2, 0, 1))
MESH = pl.DeviceIdType.MESH


def device_at(x, y, z, core):
    return ((y // 2) * 8 + z * 2 + core, (y % 2) * 4 + x)


def send(src, dst, ssem, rsem, to):
    return pltpu.make_async_remote_copy(
        src_ref=src, dst_ref=dst, send_sem=ssem, recv_sem=rsem, device_id=to, device_id_type=MESH
    )


def greet(me):
    barrier = pltpu.get_barrier_semaphore()
    x, y, z, core = me
    peers = []
    for dx in range(4):
        for dy in range(4):
            for dz in range(4):
                if (dx, dy, dz) != (0, 0, 0) and 0 in (dx, dy, dz):
                    peers.append(device_at((x + dx) % 4, (y + dy) % 4, (z + dz) % 4, core))
    for dz in range(4):
        peers.append(device_at(x, y, (z + dz) % 4, 1 - core))
    for peer in peers:
        pl.semaphore_signal(barrier, inc=1, device_id=peer, device_id_type=MESH)
    pl.semaphore_wait(barrier, len(peers))


def word_copies(dp, seq, packed, words, ws, wr):
    return [
        send(packed, words.at[seq], ws.at[d - 1], wr.at[d - 1], (dp, (seq + d) % SEQ)) for d in range(1, SEQ)
    ]


def rim_copies(dp, seq, pk, halo, hs, hr):
    return [
        send(pk.at[0], halo.at[1], hs.at[0], hr.at[0], (dp, (seq + SEQ - 1) % SEQ)),
        send(pk.at[1], halo.at[0], hs.at[1], hr.at[1], (dp, (seq + 1) % SEQ)),
    ]


def pack_part(p, me, unit_s, own, oth):
    core = me[3]
    for j in range(64):
        at = [0, 0, 0]
        at[ORDER[p][0]], at[ORDER[p][1]], at[ORDER[p][2]] = j // 16, (j // 4) % 4, j % 4
        x, y, z = at
        unit = (y // 2) * 8 + z * 2
        r0 = p * 256 + x * 64 + (y % 2) * 32
        own[p, j] = unit_s[unit + core, r0 : r0 + 32, :].astype(BF16)
        oth[p, j] = unit_s[unit + 1 - core, r0 : r0 + 32, :].astype(BF16)


def pair_copy(p, me, oth, recv_d, ss, rs):
    x, y, z, core = me
    return send(oth.at[p], recv_d.at[p], ss.at[p], rs.at[p], device_at(x, y, z, 1 - core))


def pair_sum(p, own, recv_d):
    for j in range(0, 64, 4):
        own[p, j : j + 4] = own[p, j : j + 4] + recv_d[p, j : j + 4]


def ring_copies(p, me, own, recv_1, ss, rs):
    axis = ORDER[p][0]
    out = []
    for d in range(1, 4):
        to = list(me)
        to[axis] = (me[axis] + d) % 4
        src = own.at[p, pl.ds(to[axis] * 16, 16)]
        out.append(send(src, recv_1.at[p, d - 1], ss.at[p, d - 1], rs.at[p, d - 1], device_at(*to)))
    return out


def ring_sum(p, me, own, recv_1, buf_2):
    base = me[ORDER[p][0]] * 16
    for j in range(16):
        total = own[p, base + j].astype(F32)
        for d in range(3):
            total = total + recv_1[p, d, j].astype(F32)
        buf_2[p, j] = total.astype(BF16)


def plane_copies(p, me, buf_2, recv_2, ss, rs):
    b, c = ORDER[p][1], ORDER[p][2]
    out = []
    for e in range(1, 16):
        to = list(me)
        to[b] = (me[b] + e // 4) % 4
        to[c] = (me[c] + e % 4) % 4
        src = buf_2.at[p, to[b] * 4 + to[c]]
        out.append(send(src, recv_2.at[p, e - 1], ss.at[p, e - 1], rs.at[p, e - 1], device_at(*to)))
    return out


def plane_sum(p, me, buf_2, recv_2, fin):
    total = buf_2[p, me[ORDER[p][1]] * 4 + me[ORDER[p][2]]].astype(F32)
    for e in range(15):
        total = total + recv_2[p, e].astype(F32)
    fin[p] = total.astype(BF16)


def share_copies(dp, seq, fin, gath, ss, rs):
    return [
        send(fin, gath.at[seq], ss.at[d - 1], rs.at[d - 1], (dp, (seq + d) % SEQ)) for d in range(1, SEQ)
    ]


def place_tower(gath, flat, tower_ref):
    for s in range(SEQ):
        for p in range(3):
            r0 = p * 256 + (s % 4) * 64 + (s // 4) * 32
            flat[r0 : r0 + 32, :] = gath[s, p].astype(F32)
    for i, t in enumerate(TAPS):
        for ct in range(4):
            j = 4 * i + ct
            tower_ref[t, :, ct * 128 : (ct + 1) * 128] = flat[38 * j : 38 * j + 38, :]


def pack_stem(stem_acc, gain_acc, gain, stb):
    even = stem_acc[0:C1, :]
    odd = jnp.concatenate([stem_acc[C1:, 4:64], stem_acc[C1:, 0:4]], axis=1)
    lane = lax.broadcasted_iota(I32, (C1, 64), 1)
    total = jnp.sum(gain_acc[...], axis=1, keepdims=True)
    both = jnp.where(lane < 60, even + odd, jnp.where(lane == 60, total, 0.0)).T
    row = lax.broadcasted_iota(I32, (8, 1), 0)
    last = jnp.where(row == 4, both[56:64] * (4.0 / gain[...]), both[56:64])
    for i in range(16):
        cols = slice((i // 8) * 256, (i // 8) * 256 + 256)
        stb[i] = last[:, cols] if i % 8 == 7 else both[(i % 8) * 8 : (i % 8) * 8 + 8, cols]


def stem_plane_copies(me, src_of, recv, slot_of, ss, rs):
    x, y, z, core = me
    out = []
    for e in range(1, 16):
        tx, ty = (x + e // 4) % 4, (y + e % 4) % 4
        out.append(
            send(src_of(tx * 4 + ty), recv.at[slot_of(e)], ss.at[e - 1], rs.at[e - 1], device_at(tx, ty, z, core))
        )
    return out


def stem_line_copies(me, piece, recv, ss, rs):
    x, y, z, core = me
    out = []
    for e in range(1, 8):
        to = device_at(x, y, (z + e // 2) % 4, (core + e % 2) % 2)
        out.append(send(piece, recv.at[z * 2 + core], ss.at[e - 1], rs.at[e - 1], to))
    return out


def place_stem(gath, stem_ref, gain_ref):
    for half in range(2):
        cols = slice(half * 256, half * 256 + 256)
        for s in range(K1):
            r = 4 * s
            stem_ref[s, :, cols] = gath[half * 8 + r // 8, r % 8 : r % 8 + 4, :]
        gain_ref[:, cols] = gath[half * 8 + 7, 4:5, :]


def start(copies):
    for c in copies:
        c.start()


def wait(copies):
    for c in copies:
        c.wait()


def whole_kernel(
    packed, rc_ref, sh_ref, cot_hbm, sw_ref, gain, w_hbm,
    resp_hbm, stem_ref, gain_ref, tower_ref,
    cot_v, w5, sw_f, wcat, gain_b, wt, gt, oh, act, xt,
    stem_s, ag, fac, sg_s, gain_acc, stem_acc, tg_s, unit_s,
    words, edge, pk, halo, rim, own, oth, recv_d, recv_1, buf_2, recv_2, fin, gath, flat,
    stb, recv_a, piece_a, recv_b, piece_b, gath_a,
    sems, ws, wr, hs, hr, ds, dr, s1, r1, s2, r2, s3, r3, sa, ra, sb, rb, sg, rg,
):
    dp, seq = lax.axis_index("dp"), lax.axis_index("seq")
    x, y, z, core = seq % 4, (dp // 8) * 2 + seq // 4, (dp // 2) % 4, dp % 2
    me = (x, y, z, core)
    ends = [
        pltpu.make_async_copy(cot_hbm.at[:, 0:128], edge.at[0], sems.at[9]),
        pltpu.make_async_copy(cot_hbm.at[:, ROWS - 128 : ROWS], edge.at[1], sems.at[10]),
    ]
    cuts = (0, 160, 320, 464, F2)
    cots = [
        pltpu.make_async_copy(
            cot_hbm.at[cuts[i] : cuts[i + 1], :], cot_v.at[cuts[i] : cuts[i + 1], :], sems.at[i]
        )
        for i in range(4)
    ]
    weights = [pltpu.make_async_copy(w_hbm.at[t], w5.at[t], sems.at[4 + t]) for t in range(K2)]
    start(ends)
    start(cots)
    start(weights)
    greet(me)
    edges = word_copies(dp, seq, packed, words, ws, wr)
    start(edges)
    for i in range(2):
        ends[i].wait()
        pk[i] = edge[i].T[0:16] if i == 0 else edge[i].T[112:128]
    rims = rim_copies(dp, seq, pk, halo, hs, hr)
    start(rims)
    words[seq] = packed[...]
    gain_acc[...] = jnp.zeros_like(gain_acc)
    stem_acc[...] = jnp.zeros_like(stem_acc)
    unit_s[:, 760:768, :] = jnp.zeros((16, 8, 128), F32)
    prep_stem_weight(sw_ref, sw_f, wcat, gain, gain_b)
    wait(cots)
    prep_cot(cot_v, gt)
    wait(weights)
    prep_tower_weight(w5, wt)
    for n in range(1, 4):
        ag_chunk(n, wt, gt, ag)
    wait(edges)
    decode(words, rc_ref[0], sh_ref[0], seq, oh)
    for n in range(8):
        stem_chunk(n, wcat, oh, stem_s)
        if n < 3:
            ag_chunk(n + 4, wt, gt, ag)
        pool_chunk(n, seq, stem_s, gain_b, act, fac)

    def tap(i):
        if i != 0:
            shift_act(TAPS[i], act, xt)
        tower_tap(i, cot_v, act, xt, tg_s, unit_s)

    pairs, rings, planes = [], [], []

    def pair(p):
        pack_part(p, me, unit_s, own, oth)
        pairs.append(pair_copy(p, me, oth, recv_d, ds, dr))
        pairs[p].start()

    def ring(p):
        pairs[p].wait()
        pair_sum(p, own, recv_d)
        rings.append(ring_copies(p, me, own, recv_1, s1, r1))
        start(rings[p])

    def plane(p):
        wait(rings[p])
        ring_sum(p, me, own, recv_1, buf_2)
        planes.append(plane_copies(p, me, buf_2, recv_2, s2, r2))
        start(planes[p])

    def resp(n):
        resp_chunk(n, w5, act, xt, cot_v)

    tap(0)
    tap(1)
    pair(0)
    tap(2)
    ring(0)
    tap(3)
    pair(1)
    tap(4)
    pair(2)
    wait(rims)
    rim_cot(cot_v, halo, seq, rim, gt)
    ag_chunk(0, wt, gt, ag)
    ring(1)
    ag_chunk(7, wt, gt, ag)
    for n in range(8):
        back_chunk(n, ag, fac, sg_s, gain_acc)
        stem_grad_chunk(n, sg_s, oh, stem_acc)
    ring(2)
    pack_stem(stem_acc, gain_acc, gain, stb)
    level_a = stem_plane_copies(me, lambda a: stb.at[a], recv_a, lambda e: e - 1, sa, ra)
    start(level_a)
    resp(0)
    resp(1)
    plane(0)
    resp(2)
    wait(level_a)
    total = stb[x * 4 + y]
    for e in range(15):
        total = total + recv_a[e]
    piece_a[...] = total
    recv_b[z * 2 + core] = total
    level_b = stem_line_copies(me, piece_a, recv_b, sb, rb)
    start(level_b)
    resp(3)
    resp(4)
    plane(1)
    wait(level_b)
    total = recv_b[0]
    for e in range(1, 8):
        total = total + recv_b[e]
    piece_b[...] = total
    gath_a[x * 4 + y] = total
    level_c = stem_plane_copies(me, lambda a: piece_b, gath_a, lambda e: x * 4 + y, sg, rg)
    start(level_c)
    resp(5)
    resp(6)
    plane(2)
    resp(7)
    c3 = pltpu.make_async_copy(cot_v, resp_hbm, sems.at[0])
    c3.start()
    for p in range(3):
        wait(planes[p])
        plane_sum(p, me, buf_2, recv_2, fin)
    share = share_copies(dp, seq, fin, gath, s3, r3)
    start(share)
    gath[seq] = fin[...]
    wait(level_c)
    place_stem(gath_a, stem_ref, gain_ref)
    c3.wait()
    wait(share)
    place_tower(gath, flat, tower_ref)


def scratch():
    V = pltpu.VMEM
    D = pltpu.SemaphoreType.DMA
    return [
        V((F2, ROWS), BF16),
        V((K2, F2, C1), BF16),
        V((128, C1), F32),
        V((2 * C1, 128), BF16),
        V((C1, 128), F32),
        V((C1, KF), BF16),
        V((KF, ROWS), BF16),
        V((128, WIDE), BF16),
        V((C1, WIDE), BF16),
        V((K2 - 1, C1, ROWS), BF16),
        V((2, 2 * C1, CH), F32),
        V((C1, ROWS), BF16),
        V((3, C1, ROWS), BF16),
        V((2, 2 * C1, CH), BF16),
        V((C1, 128), F32),
        V((2 * C1, 64), F32),
        V((2, F2, C1), F32),
        V((16, UNIT, 128), F32),
        V((SEQ, 1, 256), I32),
        V((2, F2, 128), BF16),
        V((2, 16, F2), BF16),
        V((2, 16, F2), BF16),
        V((F2, 128), BF16),
        V((3, 64, 32, 128), BF16),
        V((3, 64, 32, 128), BF16),
        V((3, 64, 32, 128), BF16),
        V((3, 3, 16, 32, 128), BF16),
        V((3, 16, 32, 128), BF16),
        V((3, 15, 32, 128), BF16),
        V((3, 32, 128), BF16),
        V((SEQ, 3, 32, 128), BF16),
        V((UNIT, 128), F32),
        V((16, 8, 256), F32),
        V((15, 8, 256), F32),
        V((8, 256), F32),
        V((8, 8, 256), F32),
        V((8, 256), F32),
        V((16, 8, 256), F32),
        D((11,)), D((7,)), D((7,)), D((2,)), D((2,)), D((3,)), D((3,)),
        D((3, 3)), D((3, 3)), D((3, 15)), D((3, 15)), D((7,)), D((7,)),
        D((15,)), D((15,)), D((7,)), D((7,)), D((15,)), D((15,)),
    ]


def hand_over(resp, stem, gain, tower, resp_o, stem_o, gain_o, tower_o, sems):
    cuts = (0, 160, 320, 464, F2)
    copies = [
        pltpu.make_async_copy(resp.at[cuts[i] : cuts[i + 1], :], resp_o.at[cuts[i] : cuts[i + 1], :], sems.at[i])
        for i in range(4)
    ]
    for i, (src, dst) in enumerate(((stem, stem_o), (gain, gain_o), (tower, tower_o))):
        copies.append(pltpu.make_async_copy(src, dst, sems.at[4 + i]))
    start(copies)
    wait(copies)


def shards(packed, rc_flags, shifts, cotangent, stem_weight, pool_gain, tower_weight):
    S = pl.BlockSpec(memory_space=pltpu.SMEM)
    VM = pl.BlockSpec(memory_space=pltpu.VMEM)
    A = pl.BlockSpec(memory_space=pl.ANY)
    resp, stem, gain, tower = pl.pallas_call(
        whole_kernel,
        out_shape=(
            jax.ShapeDtypeStruct((F2, ROWS), BF16),
            jax.ShapeDtypeStruct((K1, 4, C1), F32),
            jax.ShapeDtypeStruct((1, C1), F32),
            jax.ShapeDtypeStruct((K2, 38, C1), F32),
        ),
        in_specs=[VM, S, S, A, VM, VM, A],
        out_specs=(A, VM, VM, VM),
        scratch_shapes=scratch(),
        compiler_params=pltpu.CompilerParams(
            vmem_limit_bytes=62 * 1024 * 1024, collective_id=0, has_side_effects=True
        ),
    )(
        packed, rc_flags, shifts, cotangent[0].T, stem_weight, pool_gain[None],
        jnp.transpose(tower_weight, (1, 0, 2)),
    )
    resp, stem, gain, tower = pl.pallas_call(
        hand_over,
        out_shape=tuple(jax.ShapeDtypeStruct(v.shape, v.dtype) for v in (resp, stem, gain, tower)),
        in_specs=[A] * 4,
        out_specs=(A,) * 4,
        scratch_shapes=[pltpu.SemaphoreType.DMA((7,))],
    )(resp, stem, gain, tower)
    return resp.T[None], stem, gain[0], jnp.transpose(tower, (1, 0, 2))


def solution(mesh):
    in_specs = (P("dp", "seq"), P("dp"), P("dp"), P("dp", "seq", None), P(), P(), P())
    out_specs = (P("dp", "seq", None), P(), P(), P("dp", None, None))
    return jax.shard_map(shards, mesh=mesh, in_specs=in_specs, out_specs=out_specs, check_vma=False)
```

```python
import functools
import jax
import jax.numpy as jnp
from jax import lax
from jax.experimental import pallas as pl
from jax.experimental.pallas import tpu as pltpu
from jax.sharding import PartitionSpec as P

F32, BF16, I32 = jnp.float32, jnp.bfloat16, jnp.int32
C1, F2, K1, K2 = 512, 608, 15, 5
ROWS = 1920
WIDE = 2048
KF = 3072
UNIT = 768
SEQ = 8
CH = 256


def dot(a, b):
    return lax.dot_general(a, b, (((1,), (0,)), ((), ())), preferred_element_type=F32)


def dot_nt(a, b):
    return lax.dot_general(a, b, (((1,), (1,)), ((), ())), preferred_element_type=F32)


def prep_stem_weight(sw_ref, sw_f, wcat, gain, gain_b):
    sw_f[60:68, :] = jnp.zeros((8, C1), F32)
    for s in range(K1):
        v = sw_ref[s].astype(F32) * 0.25
        sw_f[4 * s : 4 * s + 4, :] = v
        sw_f[68 + 4 * s : 72 + 4 * s, :] = v
    w = sw_f[...].T
    lane = lax.broadcasted_iota(I32, (C1, 128), 1)
    wcat[0:C1, :] = jnp.where(lane < 64, w, -w).astype(BF16)
    wcat[C1:, :] = w.astype(BF16)
    gain_b[...] = jnp.broadcast_to(gain[...], (128, C1)).T * 2.0


def prep_tower_weight(w5, wt):
    flat = w5.reshape(K2 * F2, C1)

    def block(i, _):
        r0 = pl.multiple_of(i * 128, 128)
        wt[:, pl.ds(r0, 128)] = flat[pl.ds(r0, 128), :].T
        return 0

    lax.fori_loop(0, (K2 * F2) // 128, block, 0, unroll=True)
    tail = K2 * F2 - (K2 * F2) // 128 * 128
    v = jnp.concatenate([flat[K2 * F2 - tail :, :], jnp.zeros((128 - tail, C1), BF16)], axis=0)
    wt[:, KF - 128 :] = v.T


def prep_cot(cot_v, gt):
    def rows(i, _):
        r0 = pl.multiple_of(i * 16, 16)
        full = cot_v[pl.ds(r0, 16), :]
        for t in range(K2):
            s = 2 - t
            v = full if s == 0 else pltpu.roll(full, (-s) % ROWS, 1)
            gt[pl.ds(pl.multiple_of(t * F2 + r0, 16), 16), :] = v
        return 0

    lax.fori_loop(0, F2 // 16, rows, 0, unroll=True)
    gt[K2 * F2 : KF, :] = jnp.zeros((KF - K2 * F2, ROWS), BF16)


def rim_cot(cot_v, halo, seq, rim, gt):
    nxt = jnp.where(seq < SEQ - 1, halo[1].astype(F32), 0.0)
    prv = jnp.where(seq > 0, halo[0].astype(F32), 0.0)
    rim[...] = jnp.concatenate([nxt, jnp.zeros((96, F2), F32), prv], axis=0).T.astype(BF16)
    for r in range(0, F2, 16):
        rs = slice(r, r + 16)
        ring = jnp.concatenate([cot_v[rs, ROWS - 256 : ROWS], rim[rs, :], cot_v[rs, 0:256]], axis=1)
        for t in range(K2):
            s = 2 - t
            if s != 0:
                v = pltpu.roll(ring, (-s) % 640, 1)
                gt[t * F2 + r : t * F2 + r + 16, ROWS - 128 : ROWS] = v[:, 128:256]
                gt[t * F2 + r : t * F2 + r + 16, 0:128] = v[:, 384:512]


def decode(words, rc, shift, seq, oh):
    take = jnp.where(rc == 1, SEQ - 1 - seq, seq)
    slot = lax.broadcasted_iota(I32, (SEQ, 1, CH), 0)
    w8 = words[...]
    own = jnp.sum(jnp.where(slot == take, w8, 0), axis=0)
    low = jnp.sum(jnp.where(slot == take - 1, w8, 0), axis=0)
    high = jnp.sum(jnp.where(slot == take + 1, w8, 0), axis=0)
    lane = lax.broadcasted_iota(I32, (1, 128), 1)
    rim = jnp.where(lane == 127, low[:, 128:256], jnp.where(lane == 0, high[:, 0:128], 0))
    row = jnp.broadcast_to(jnp.concatenate([own, rim], axis=1), (8, 384))
    after = jnp.where(rc == 1, pltpu.roll(row, 1, 1), pltpu.roll(row, 383, 1))
    sub = lax.broadcasted_iota(I32, (8, 384), 0)
    planes = (jnp.where(sub < 4, row, after) >> (8 * (sub & 3))) & 255
    planes = planes.astype(F32).astype(BF16)
    src = lax.broadcasted_iota(I32, (384, CH), 0)
    src = jnp.where(src == 383, -1, src)
    part = lax.broadcasted_iota(I32, (64, CH), 0)
    s = part >> 2
    want = jnp.where(rc == 1, 3 - (part & 3), part & 3)

    def chunk(i, _):
        u0 = pl.multiple_of(i * CH, CH)
        u = u0 + lax.broadcasted_iota(I32, (1, CH), 1)
        q = jnp.where(u < 1984, u, u - WIDE)
        b0 = 2 * q - 7 - shift
        j0 = (((b0 + 30) * 34953) >> 19) - 2
        i0 = b0 - 15 * j0
        at = jnp.where(rc == 1, 255 - j0, j0)
        sel = jnp.where(src == at, 1.0, 0.0).astype(BF16)
        got = dot(planes, sel).astype(I32)
        word_a = got[0:1] + (got[1:2] << 8) + (got[2:3] << 16) + (got[3:4] << 24)
        word_b = got[4:5] + (got[5:6] << 8) + (got[6:7] << 16) + (got[7:8] << 24)
        d = i0 + s
        late = d >= 15
        word = jnp.where(late, word_b, word_a)
        d = jnp.where(late, d - 15, d)
        d = jnp.where(rc == 1, 14 - d, d)
        where = 2 * ROWS * seq + b0 + s
        good = (where >= 0) & (where < 2 * ROWS * SEQ)
        hit = (((word >> (2 * d)) & 3) == want) & good
        hot = jnp.where(hit, 1.0, 0.0).astype(BF16)
        oh[0:64, pl.ds(u0, CH)] = hot
        oh[64:128, pl.ds(u0, CH)] = hot
        return 0

    lax.fori_loop(0, WIDE // CH, chunk, 0, unroll=True)


GELU_A = 0.7978845608028654
GELU_B = 0.044715


def pool(hd, mean, gain2):
    gd = gain2 * hd
    t = jnp.tanh(gd)
    hx = mean + t * hd
    h2 = hx * hx
    th = jnp.tanh(hx * (2 * GELU_A + (8 * GELU_A * GELU_B) * h2))
    p1 = 1.0 + th
    act = hx * p1
    dgelu = p1 * (0.25 + hx * (2.0 - p1) * (0.5 * GELU_A + (6 * GELU_A * GELU_B) * h2))
    k = gd * (1.0 - t * t)
    m1 = (1.0 + t) + k
    return act, dgelu * m1, dgelu * (2.0 - m1), dgelu * (hd * k)


def span(n):
    return slice(n * CH, min((n + 1) * CH, ROWS))


def ag_chunk(n, wt, gt, ag):
    ag[:, span(n)] = dot(wt[...], gt[:, span(n)]).astype(BF16)


def stem_chunk(n, wcat, oh, stem_s):
    stem_s[n % 2] = dot(wcat[...], oh[:, n * CH : (n + 1) * CH])


def pool_chunk(n, seq, stem_s, gain_b, act, fac):
    for r in range(0, C1, 16):
        for lt in range(2):
            cols = slice(lt * 128, lt * 128 + 128)
            at = slice(n * CH + lt * 128, n * CH + lt * 128 + 128)
            a, f1, f2, f3 = pool(
                stem_s[n % 2, r : r + 16, cols], stem_s[n % 2, C1 + r : C1 + r + 16, cols], gain_b[r : r + 16, :]
            )
            if at.start >= ROWS:
                lane = lax.broadcasted_iota(I32, (16, 128), 1)
                out = ((lane < 64) & (seq == SEQ - 1)) | ((lane >= 64) & (seq == 0))
                a = jnp.where(out, 0.0, a)
            else:
                fac[0, r : r + 16, at] = f1.astype(BF16)
                fac[1, r : r + 16, at] = f2.astype(BF16)
                fac[2, r : r + 16, at] = f3.astype(BF16)
            act[r : r + 16, at] = a.astype(BF16)


def back_chunk(n, ag, fac, sg_s, gain_acc):
    for r in range(0, C1, 16):
        for c0 in range(span(n).start, span(n).stop, 128):
            rs, cs = slice(r, r + 16), slice(c0, c0 + 128)
            o = slice(c0 % CH, c0 % CH + 128)
            g = ag[rs, cs]
            sg_s[n % 2, rs, o] = g * fac[0, rs, cs]
            sg_s[n % 2, C1 + r : C1 + r + 16, o] = g * fac[1, rs, cs]
            gain_acc[rs, :] += g.astype(F32) * fac[2, rs, cs].astype(F32)


def stem_grad_chunk(n, sg_s, oh, stem_acc):
    w = span(n).stop - span(n).start
    stem_acc[...] += dot_nt(sg_s[n % 2, :, 0:w], oh[0:64, span(n)])


def shift_act(t, act, xt):
    s = t - 2
    for r in range(0, C1, 16):
        v = pltpu.roll(act[r : r + 16, :], (-s) % WIDE, 1)
        xt[t - t // 3, r : r + 16, :] = v[:, 0:ROWS]


TAPS = (2, 1, 3, 0, 4)


def tower_tap(i, cot_v, act, xt, tg_s, unit_s):
    t = TAPS[i]
    rhs = act[:, 0:ROWS] if t == 2 else xt[t - t // 3]
    tg_s[i % 2] = dot_nt(cot_v[...], rhs)
    for d in range(16):
        for ct in range(4):
            piece = tg_s[i % 2, 38 * d : 38 * d + 38, ct * 128 : (ct + 1) * 128]
            unit_s[d, 152 * i + 38 * ct : 152 * i + 38 * ct + 38, :] = piece


def resp_chunk(n, w5, act, xt, resp_v):
    cols = span(n)
    taps = jnp.concatenate([w5[t] for t in range(K2)], axis=1)
    rhs = jnp.concatenate([act[:, cols] if t == 2 else xt[t - t // 3, :, cols] for t in range(K2)], axis=0)
    resp_v[:, cols] = dot(taps, rhs).astype(BF16)


ORDER = ((0, 1, 2), (1, 2, 0), (2, 0, 1))
MESH = pl.DeviceIdType.MESH


def device_at(x, y, z, core):
    return ((y // 2) * 8 + z * 2 + core, (y % 2) * 4 + x)


def send(src, dst, ssem, rsem, to):
    return pltpu.make_async_remote_copy(
        src_ref=src, dst_ref=dst, send_sem=ssem, recv_sem=rsem, device_id=to, device_id_type=MESH
    )


def greet(me):
    barrier = pltpu.get_barrier_semaphore()
    x, y, z, core = me
    peers = []
    for dx in range(4):
        for dy in range(4):
            for dz in range(4):
                if (dx, dy, dz) != (0, 0, 0) and 0 in (dx, dy, dz):
                    peers.append(device_at((x + dx) % 4, (y + dy) % 4, (z + dz) % 4, core))
    for dz in range(4):
        peers.append(device_at(x, y, (z + dz) % 4, 1 - core))
    for peer in peers:
        pl.semaphore_signal(barrier, inc=1, device_id=peer, device_id_type=MESH)
    pl.semaphore_wait(barrier, len(peers))


def word_copies(dp, seq, packed, words, ws, wr):
    return [
        send(packed, words.at[seq], ws.at[d - 1], wr.at[d - 1], (dp, (seq + d) % SEQ)) for d in range(1, SEQ)
    ]


def rim_copies(dp, seq, pk, halo, hs, hr):
    return [
        send(pk.at[0], halo.at[1], hs.at[0], hr.at[0], (dp, (seq + SEQ - 1) % SEQ)),
        send(pk.at[1], halo.at[0], hs.at[1], hr.at[1], (dp, (seq + 1) % SEQ)),
    ]


def pack_part(p, me, unit_s, own, oth):
    core = me[3]
    for j in range(64):
        at = [0, 0, 0]
        at[ORDER[p][0]], at[ORDER[p][1]], at[ORDER[p][2]] = j // 16, (j // 4) % 4, j % 4
        x, y, z = at
        unit = (y // 2) * 8 + z * 2
        r0 = p * 256 + x * 64 + (y % 2) * 32
        own[p, j] = unit_s[unit + core, r0 : r0 + 32, :].astype(BF16)
        oth[p, j] = unit_s[unit + 1 - core, r0 : r0 + 32, :].astype(BF16)


def pair_copy(p, me, oth, recv_d, ss, rs):
    x, y, z, core = me
    return send(oth.at[p], recv_d.at[p], ss.at[p], rs.at[p], device_at(x, y, z, 1 - core))


def pair_sum(p, own, recv_d):
    for j in range(0, 64, 4):
        own[p, j : j + 4] = own[p, j : j + 4] + recv_d[p, j : j + 4]


def ring_copies(p, me, own, recv_1, ss, rs):
    axis = ORDER[p][0]
    out = []
    for d in range(1, 4):
        to = list(me)
        to[axis] = (me[axis] + d) % 4
        src = own.at[p, pl.ds(to[axis] * 16, 16)]
        out.append(send(src, recv_1.at[p, d - 1], ss.at[p, d - 1], rs.at[p, d - 1], device_at(*to)))
    return out


def ring_sum(p, me, own, recv_1, buf_2):
    base = me[ORDER[p][0]] * 16
    for j in range(16):
        total = own[p, base + j].astype(F32)
        for d in range(3):
            total = total + recv_1[p, d, j].astype(F32)
        buf_2[p, j] = total.astype(BF16)


def plane_copies(p, me, buf_2, recv_2, ss, rs):
    b, c = ORDER[p][1], ORDER[p][2]
    out = []
    for e in range(1, 16):
        to = list(me)
        to[b] = (me[b] + e // 4) % 4
        to[c] = (me[c] + e % 4) % 4
        src = buf_2.at[p, to[b] * 4 + to[c]]
        out.append(send(src, recv_2.at[p, e - 1], ss.at[p, e - 1], rs.at[p, e - 1], device_at(*to)))
    return out


def plane_sum(p, me, buf_2, recv_2, fin):
    total = buf_2[p, me[ORDER[p][1]] * 4 + me[ORDER[p][2]]].astype(F32)
    for e in range(15):
        total = total + recv_2[p, e].astype(F32)
    fin[p] = total.astype(BF16)


def share_copies(dp, seq, fin, gath, ss, rs):
    return [
        send(fin, gath.at[seq], ss.at[d - 1], rs.at[d - 1], (dp, (seq + d) % SEQ)) for d in range(1, SEQ)
    ]


def place_tower(gath, flat, tower_ref):
    for s in range(SEQ):
        for p in range(3):
            r0 = p * 256 + (s % 4) * 64 + (s // 4) * 32
            flat[r0 : r0 + 32, :] = gath[s, p].astype(F32)
    for i, t in enumerate(TAPS):
        for ct in range(4):
            j = 4 * i + ct
            tower_ref[t, :, ct * 128 : (ct + 1) * 128] = flat[38 * j : 38 * j + 38, :]


def pack_stem(stem_acc, gain_acc, gain, stb):
    even = stem_acc[0:C1, :]
    odd = jnp.concatenate([stem_acc[C1:, 4:64], stem_acc[C1:, 0:4]], axis=1)
    lane = lax.broadcasted_iota(I32, (C1, 64), 1)
    total = jnp.sum(gain_acc[...], axis=1, keepdims=True)
    both = jnp.where(lane < 60, even + odd, jnp.where(lane == 60, total, 0.0)).T
    row = lax.broadcasted_iota(I32, (8, 1), 0)
    last = jnp.where(row == 4, both[56:64] * (4.0 / gain[...]), both[56:64])
    for i in range(16):
        cols = slice((i // 8) * 256, (i // 8) * 256 + 256)
        stb[i] = last[:, cols] if i % 8 == 7 else both[(i % 8) * 8 : (i % 8) * 8 + 8, cols]


def stem_plane_copies(me, src_of, recv, slot_of, ss, rs):
    x, y, z, core = me
    out = []
    for e in range(1, 16):
        tx, ty = (x + e // 4) % 4, (y + e % 4) % 4
        out.append(
            send(src_of(tx * 4 + ty), recv.at[slot_of(e)], ss.at[e - 1], rs.at[e - 1], device_at(tx, ty, z, core))
        )
    return out


def stem_line_copies(me, piece, recv, ss, rs):
    x, y, z, core = me
    out = []
    for e in range(1, 8):
        to = device_at(x, y, (z + e // 2) % 4, (core + e % 2) % 2)
        out.append(send(piece, recv.at[z * 2 + core], ss.at[e - 1], rs.at[e - 1], to))
    return out


def place_stem(gath, stem_ref, gain_ref):
    for half in range(2):
        cols = slice(half * 256, half * 256 + 256)
        for s in range(K1):
            r = 4 * s
            stem_ref[s, :, cols] = gath[half * 8 + r // 8, r % 8 : r % 8 + 4, :]
        gain_ref[:, cols] = gath[half * 8 + 7, 4:5, :]


def start(copies):
    for c in copies:
        c.start()


def wait(copies):
    for c in copies:
        c.wait()


def whole_kernel(
    packed, rc_ref, sh_ref, cot_hbm, sw_ref, gain, w_hbm,
    resp_hbm, stem_ref, gain_ref, tower_ref,
    cot_v, w5, sw_f, wcat, gain_b, wt, gt, oh, act, xt,
    stem_s, ag, fac, sg_s, gain_acc, stem_acc, tg_s, unit_s,
    words, edge, pk, halo, rim, own, oth, recv_d, recv_1, buf_2, recv_2, fin, gath, flat,
    stb, recv_a, piece_a, recv_b, piece_b, gath_a,
    sems, ws, wr, hs, hr, ds, dr, s1, r1, s2, r2, s3, r3, sa, ra, sb, rb, sg, rg,
):
    dp, seq = lax.axis_index("dp"), lax.axis_index("seq")
    x, y, z, core = seq % 4, (dp // 8) * 2 + seq // 4, (dp // 2) % 4, dp % 2
    me = (x, y, z, core)
    ends = [
        pltpu.make_async_copy(cot_hbm.at[:, 0:128], edge.at[0], sems.at[9]),
        pltpu.make_async_copy(cot_hbm.at[:, ROWS - 128 : ROWS], edge.at[1], sems.at[10]),
    ]
    cuts = (0, 160, 320, 464, F2)
    cots = [
        pltpu.make_async_copy(
            cot_hbm.at[cuts[i] : cuts[i + 1], :], cot_v.at[cuts[i] : cuts[i + 1], :], sems.at[i]
        )
        for i in range(4)
    ]
    weights = [pltpu.make_async_copy(w_hbm.at[t], w5.at[t], sems.at[4 + t]) for t in range(K2)]
    start(ends)
    start(cots)
    start(weights)
    greet(me)
    edges = word_copies(dp, seq, packed, words, ws, wr)
    start(edges)
    for i in range(2):
        ends[i].wait()
        pk[i] = edge[i].T[0:16] if i == 0 else edge[i].T[112:128]
    rims = rim_copies(dp, seq, pk, halo, hs, hr)
    start(rims)
    words[seq] = packed[...]
    gain_acc[...] = jnp.zeros_like(gain_acc)
    stem_acc[...] = jnp.zeros_like(stem_acc)
    unit_s[:, 760:768, :] = jnp.zeros((16, 8, 128), F32)
    prep_stem_weight(sw_ref, sw_f, wcat, gain, gain_b)
    wait(cots)
    prep_cot(cot_v, gt)
    wait(weights)
    prep_tower_weight(w5, wt)
    for n in range(1, 4):
        ag_chunk(n, wt, gt, ag)
    wait(edges)
    decode(words, rc_ref[0], sh_ref[0], seq, oh)
    for n in range(8):
        stem_chunk(n, wcat, oh, stem_s)
        if n < 3:
            ag_chunk(n + 4, wt, gt, ag)
        pool_chunk(n, seq, stem_s, gain_b, act, fac)

    def tap(i):
        if i != 0:
            shift_act(TAPS[i], act, xt)
        tower_tap(i, cot_v, act, xt, tg_s, unit_s)

    pairs, rings, planes = [], [], []

    def pair(p):
        pack_part(p, me, unit_s, own, oth)
        pairs.append(pair_copy(p, me, oth, recv_d, ds, dr))
        pairs[p].start()

    def ring(p):
        pairs[p].wait()
        pair_sum(p, own, recv_d)
        rings.append(ring_copies(p, me, own, recv_1, s1, r1))
        start(rings[p])

    def plane(p):
        wait(rings[p])
        ring_sum(p, me, own, recv_1, buf_2)
        planes.append(plane_copies(p, me, buf_2, recv_2, s2, r2))
        start(planes[p])

    def resp(n):
        resp_chunk(n, w5, act, xt, cot_v)

    tap(0)
    tap(1)
    pair(0)
    tap(2)
    ring(0)
    tap(3)
    pair(1)
    tap(4)
    pair(2)
    ring(1)
    wait(rims)
    rim_cot(cot_v, halo, seq, rim, gt)
    ag_chunk(0, wt, gt, ag)
    ring(2)
    ag_chunk(7, wt, gt, ag)
    for n in range(8):
        back_chunk(n, ag, fac, sg_s, gain_acc)
        stem_grad_chunk(n, sg_s, oh, stem_acc)
    pack_stem(stem_acc, gain_acc, gain, stb)
    level_a = stem_plane_copies(me, lambda a: stb.at[a], recv_a, lambda e: e - 1, sa, ra)
    start(level_a)
    resp(0)
    resp(1)
    resp(2)
    plane(0)
    resp(3)
    resp(4)
    resp(5)
    plane(1)
    wait(level_a)
    total = stb[x * 4 + y]
    for e in range(15):
        total = total + recv_a[e]
    piece_a[...] = total
    recv_b[z * 2 + core] = total
    level_b = stem_line_copies(me, piece_a, recv_b, sb, rb)
    start(level_b)
    resp(6)
    plane(2)
    resp(7)
    c3 = pltpu.make_async_copy(cot_v, resp_hbm, sems.at[0])
    c3.start()
    wait(level_b)
    total = recv_b[0]
    for e in range(1, 8):
        total = total + recv_b[e]
    piece_b[...] = total
    gath_a[x * 4 + y] = total
    level_c = stem_plane_copies(me, lambda a: piece_b, gath_a, lambda e: x * 4 + y, sg, rg)
    start(level_c)
    for p in range(3):
        wait(planes[p])
        plane_sum(p, me, buf_2, recv_2, fin)
    share = share_copies(dp, seq, fin, gath, s3, r3)
    start(share)
    gath[seq] = fin[...]
    wait(level_c)
    place_stem(gath_a, stem_ref, gain_ref)
    c3.wait()
    wait(share)
    place_tower(gath, flat, tower_ref)


def scratch():
    V = pltpu.VMEM
    D = pltpu.SemaphoreType.DMA
    return [
        V((F2, ROWS), BF16),
        V((K2, F2, C1), BF16),
        V((128, C1), F32),
        V((2 * C1, 128), BF16),
        V((C1, 128), F32),
        V((C1, KF), BF16),
        V((KF, ROWS), BF16),
        V((128, WIDE), BF16),
        V((C1, WIDE), BF16),
        V((K2 - 1, C1, ROWS), BF16),
        V((2, 2 * C1, CH), F32),
        V((C1, ROWS), BF16),
        V((3, C1, ROWS), BF16),
        V((2, 2 * C1, CH), BF16),
        V((C1, 128), F32),
        V((2 * C1, 64), F32),
        V((2, F2, C1), F32),
        V((16, UNIT, 128), F32),
        V((SEQ, 1, 256), I32),
        V((2, F2, 128), BF16),
        V((2, 16, F2), BF16),
        V((2, 16, F2), BF16),
        V((F2, 128), BF16),
        V((3, 64, 32, 128), BF16),
        V((3, 64, 32, 128), BF16),
        V((3, 64, 32, 128), BF16),
        V((3, 3, 16, 32, 128), BF16),
        V((3, 16, 32, 128), BF16),
        V((3, 15, 32, 128), BF16),
        V((3, 32, 128), BF16),
        V((SEQ, 3, 32, 128), BF16),
        V((UNIT, 128), F32),
        V((16, 8, 256), F32),
        V((15, 8, 256), F32),
        V((8, 256), F32),
        V((8, 8, 256), F32),
        V((8, 256), F32),
        V((16, 8, 256), F32),
        D((11,)), D((7,)), D((7,)), D((2,)), D((2,)), D((3,)), D((3,)),
        D((3, 3)), D((3, 3)), D((3, 15)), D((3, 15)), D((7,)), D((7,)),
        D((15,)), D((15,)), D((7,)), D((7,)), D((15,)), D((15,)),
    ]


CUTS = (0, 80, 160, 240, 320, 400, 480, 544, F2)


def hand_over(resp, stem, gain, tower, resp_o, stem_o, gain_o, tower_o, resp_v, stem_v, gain_v, tower_v, si, so):
    way = [(stem, stem_v, stem_o), (gain, gain_v, gain_o), (tower, tower_v, tower_o)]
    for i in range(8):
        rows = slice(CUTS[i], CUTS[i + 1])
        way.append((resp.at[rows, :], resp_v.at[rows, :], resp_o.at[rows, :]))
    into = [pltpu.make_async_copy(w[0], w[1], si.at[i]) for i, w in enumerate(way)]
    out = [pltpu.make_async_copy(w[1], w[2], so.at[i]) for i, w in enumerate(way)]
    start(into)
    for i in range(len(way)):
        into[i].wait()
        out[i].start()
    wait(out)


def shards(packed, rc_flags, shifts, cotangent, stem_weight, pool_gain, tower_weight):
    S = pl.BlockSpec(memory_space=pltpu.SMEM)
    VM = pl.BlockSpec(memory_space=pltpu.VMEM)
    A = pl.BlockSpec(memory_space=pl.ANY)
    resp, stem, gain, tower = pl.pallas_call(
        whole_kernel,
        out_shape=(
            jax.ShapeDtypeStruct((F2, ROWS), BF16),
            jax.ShapeDtypeStruct((K1, 4, C1), F32),
            jax.ShapeDtypeStruct((1, C1), F32),
            jax.ShapeDtypeStruct((K2, 38, C1), F32),
        ),
        in_specs=[VM, S, S, A, VM, VM, A],
        out_specs=(A, VM, VM, VM),
        scratch_shapes=scratch(),
        compiler_params=pltpu.CompilerParams(
            vmem_limit_bytes=62 * 1024 * 1024, collective_id=0, has_side_effects=True
        ),
    )(
        packed, rc_flags, shifts, cotangent[0].T, stem_weight, pool_gain[None],
        jnp.transpose(tower_weight, (1, 0, 2)),
    )
    resp, stem, gain, tower = pl.pallas_call(
        hand_over,
        out_shape=tuple(jax.ShapeDtypeStruct(v.shape, v.dtype) for v in (resp, stem, gain, tower)),
        in_specs=[A] * 4,
        out_specs=(A,) * 4,
        scratch_shapes=[
            pltpu.VMEM((F2, ROWS), BF16),
            pltpu.VMEM((K1, 4, C1), F32),
            pltpu.VMEM((1, C1), F32),
            pltpu.VMEM((K2, 38, C1), F32),
            pltpu.SemaphoreType.DMA((11,)),
            pltpu.SemaphoreType.DMA((11,)),
        ],
        compiler_params=pltpu.CompilerParams(vmem_limit_bytes=60 * 1024 * 1024),
    )(resp, stem, gain, tower)
    return resp.T[None], stem, gain[0], jnp.transpose(tower, (1, 0, 2))


def solution(mesh):
    in_specs = (P("dp", "seq"), P("dp"), P("dp"), P("dp", "seq", None), P(), P(), P())
    out_specs = (P("dp", "seq", None), P(), P(), P("dp", None, None))
    return jax.shard_map(shards, mesh=mesh, in_specs=in_specs, out_specs=out_specs, check_vma=False)
```

```python
import functools
import jax
import jax.numpy as jnp
from jax import lax
from jax.experimental import pallas as pl
from jax.experimental.pallas import tpu as pltpu
from jax.sharding import PartitionSpec as P

F32, BF16, I32 = jnp.float32, jnp.bfloat16, jnp.int32
C1, F2, K1, K2 = 512, 608, 15, 5
ROWS = 1920
WIDE = 2048
KF = 3072
UNIT = 768
SEQ = 8
CH = 256


def dot(a, b):
    return lax.dot_general(a, b, (((1,), (0,)), ((), ())), preferred_element_type=F32)


def dot_nt(a, b):
    return lax.dot_general(a, b, (((1,), (1,)), ((), ())), preferred_element_type=F32)


def prep_stem_weight(sw_ref, sw_f, wcat, gain, gain_b):
    sw_f[60:68, :] = jnp.zeros((8, C1), F32)
    for s in range(K1):
        v = sw_ref[s].astype(F32) * 0.25
        sw_f[4 * s : 4 * s + 4, :] = v
        sw_f[68 + 4 * s : 72 + 4 * s, :] = v
    w = sw_f[...].T
    lane = lax.broadcasted_iota(I32, (C1, 128), 1)
    wcat[0:C1, :] = jnp.where(lane < 64, w, -w).astype(BF16)
    wcat[C1:, :] = w.astype(BF16)
    gain_b[...] = jnp.broadcast_to(gain[...], (128, C1)).T * 2.0


def prep_tower_weight(w5, wt):
    flat = w5.reshape(K2 * F2, C1)

    def block(i, _):
        r0 = pl.multiple_of(i * 128, 128)
        wt[:, pl.ds(r0, 128)] = flat[pl.ds(r0, 128), :].T
        return 0

    lax.fori_loop(0, (K2 * F2) // 128, block, 0, unroll=True)
    tail = K2 * F2 - (K2 * F2) // 128 * 128
    v = jnp.concatenate([flat[K2 * F2 - tail :, :], jnp.zeros((128 - tail, C1), BF16)], axis=0)
    wt[:, KF - 128 :] = v.T


def prep_cot(cot_v, gt):
    def rows(i, _):
        r0 = pl.multiple_of(i * 16, 16)
        full = cot_v[pl.ds(r0, 16), :]
        for t in range(K2):
            s = 2 - t
            v = full if s == 0 else pltpu.roll(full, (-s) % ROWS, 1)
            gt[pl.ds(pl.multiple_of(t * F2 + r0, 16), 16), :] = v
        return 0

    lax.fori_loop(0, F2 // 16, rows, 0, unroll=True)
    gt[K2 * F2 : KF, :] = jnp.zeros((KF - K2 * F2, ROWS), BF16)


def rim_cot(cot_v, halo, seq, rim, gt):
    nxt = jnp.where(seq < SEQ - 1, halo[1].astype(F32), 0.0)
    prv = jnp.where(seq > 0, halo[0].astype(F32), 0.0)
    rim[...] = jnp.concatenate([nxt, jnp.zeros((96, F2), F32), prv], axis=0).T.astype(BF16)
    for r in range(0, F2, 16):
        rs = slice(r, r + 16)
        ring = jnp.concatenate([cot_v[rs, ROWS - 256 : ROWS], rim[rs, :], cot_v[rs, 0:256]], axis=1)
        for t in range(K2):
            s = 2 - t
            if s != 0:
                v = pltpu.roll(ring, (-s) % 640, 1)
                gt[t * F2 + r : t * F2 + r + 16, ROWS - 128 : ROWS] = v[:, 128:256]
                gt[t * F2 + r : t * F2 + r + 16, 0:128] = v[:, 384:512]


def decode(words, rc, shift, seq, oh):
    take = jnp.where(rc == 1, SEQ - 1 - seq, seq)
    slot = lax.broadcasted_iota(I32, (SEQ, 1, CH), 0)
    w8 = words[...]
    own = jnp.sum(jnp.where(slot == take, w8, 0), axis=0)
    low = jnp.sum(jnp.where(slot == take - 1, w8, 0), axis=0)
    high = jnp.sum(jnp.where(slot == take + 1, w8, 0), axis=0)
    lane = lax.broadcasted_iota(I32, (1, 128), 1)
    rim = jnp.where(lane == 127, low[:, 128:256], jnp.where(lane == 0, high[:, 0:128], 0))
    row = jnp.broadcast_to(jnp.concatenate([own, rim], axis=1), (8, 384))
    after = jnp.where(rc == 1, pltpu.roll(row, 1, 1), pltpu.roll(row, 383, 1))
    sub = lax.broadcasted_iota(I32, (8, 384), 0)
    planes = (jnp.where(sub < 4, row, after) >> (8 * (sub & 3))) & 255
    planes = planes.astype(F32).astype(BF16)
    src = lax.broadcasted_iota(I32, (384, CH), 0)
    src = jnp.where(src == 383, -1, src)
    part = lax.broadcasted_iota(I32, (64, CH), 0)
    s = part >> 2
    want = jnp.where(rc == 1, 3 - (part & 3), part & 3)

    def chunk(i, _):
        u0 = pl.multiple_of(i * CH, CH)
        u = u0 + lax.broadcasted_iota(I32, (1, CH), 1)
        q = jnp.where(u < 1984, u, u - WIDE)
        b0 = 2 * q - 7 - shift
        j0 = (((b0 + 30) * 34953) >> 19) - 2
        i0 = b0 - 15 * j0
        at = jnp.where(rc == 1, 255 - j0, j0)
        sel = jnp.where(src == at, 1.0, 0.0).astype(BF16)
        got = dot(planes, sel).astype(I32)
        word_a = got[0:1] + (got[1:2] << 8) + (got[2:3] << 16) + (got[3:4] << 24)
        word_b = got[4:5] + (got[5:6] << 8) + (got[6:7] << 16) + (got[7:8] << 24)
        d = i0 + s
        late = d >= 15
        word = jnp.where(late, word_b, word_a)
        d = jnp.where(late, d - 15, d)
        d = jnp.where(rc == 1, 14 - d, d)
        where = 2 * ROWS * seq + b0 + s
        good = (where >= 0) & (where < 2 * ROWS * SEQ)
        hit = (((word >> (2 * d)) & 3) == want) & good
        hot = jnp.where(hit, 1.0, 0.0).astype(BF16)
        oh[0:64, pl.ds(u0, CH)] = hot
        oh[64:128, pl.ds(u0, CH)] = hot
        return 0

    lax.fori_loop(0, WIDE // CH, chunk, 0, unroll=True)


GELU_A = 0.7978845608028654
GELU_B = 0.044715


def activate(hd, mean, gain2):
    hx = mean + jnp.tanh(gain2 * hd) * hd
    th = jnp.tanh(hx * (2 * GELU_A + (8 * GELU_A * GELU_B) * (hx * hx)))
    return hx * (1.0 + th)


def factors(hd, mean, gain2):
    gd = gain2 * hd
    t = jnp.tanh(gd)
    hx = mean + t * hd
    h2 = hx * hx
    p1 = 1.0 + jnp.tanh(hx * (2 * GELU_A + (8 * GELU_A * GELU_B) * h2))
    dgelu = p1 * (0.25 + hx * (2.0 - p1) * (0.5 * GELU_A + (6 * GELU_A * GELU_B) * h2))
    k = gd * (1.0 - t * t)
    m1 = (1.0 + t) + k
    return dgelu * m1, dgelu * (2.0 - m1), dgelu * (hd * k)


def span(n):
    return slice(n * CH, min((n + 1) * CH, ROWS))


def ag_chunk(n, wt, gt, ag):
    ag[:, span(n)] = dot(wt[...], gt[:, span(n)]).astype(BF16)


def stem_chunk(n, wcat, oh, stem_s):
    stem_s[n % 2] = dot(wcat[...], oh[:, n * CH : (n + 1) * CH])


def act_chunk(n, seq, stem_s, gain_b, act):
    for r in range(0, C1, 16):
        for lt in range(2):
            cols = slice(lt * 128, lt * 128 + 128)
            at = slice(n * CH + lt * 128, n * CH + lt * 128 + 128)
            a = activate(
                stem_s[n % 2, r : r + 16, cols], stem_s[n % 2, C1 + r : C1 + r + 16, cols], gain_b[r : r + 16, :]
            )
            if at.start >= ROWS:
                lane = lax.broadcasted_iota(I32, (16, 128), 1)
                out = ((lane < 64) & (seq == SEQ - 1)) | ((lane >= 64) & (seq == 0))
                a = jnp.where(out, 0.0, a)
            act[r : r + 16, at] = a.astype(BF16)


def factor_chunk(n, stem_s, gain_b, fac):
    for r in range(0, C1, 16):
        for c0 in range(span(n).start, span(n).stop, 128):
            cols = slice(c0 % CH, c0 % CH + 128)
            made = factors(
                stem_s[n % 2, r : r + 16, cols], stem_s[n % 2, C1 + r : C1 + r + 16, cols], gain_b[r : r + 16, :]
            )
            for i in range(3):
                fac[i, r : r + 16, c0 : c0 + 128] = made[i].astype(BF16)


def back_chunk(n, ag, fac, sg_s, gain_acc):
    for r in range(0, C1, 16):
        for c0 in range(span(n).start, span(n).stop, 128):
            rs, cs = slice(r, r + 16), slice(c0, c0 + 128)
            o = slice(c0 % CH, c0 % CH + 128)
            g = ag[rs, cs]
            sg_s[n % 2, rs, o] = g * fac[0, rs, cs]
            sg_s[n % 2, C1 + r : C1 + r + 16, o] = g * fac[1, rs, cs]
            gain_acc[rs, :] += g.astype(F32) * fac[2, rs, cs].astype(F32)


def stem_grad_chunk(n, sg_s, oh, stem_acc):
    w = span(n).stop - span(n).start
    stem_acc[...] += dot_nt(sg_s[n % 2, :, 0:w], oh[0:64, span(n)])


def shift_act(t, act, xt):
    s = t - 2
    for r in range(0, C1, 16):
        v = pltpu.roll(act[r : r + 16, :], (-s) % WIDE, 1)
        xt[t - t // 3, r : r + 16, :] = v[:, 0:ROWS]


TAPS = (2, 1, 3, 0, 4)


def tower_tap(i, cot_v, act, xt, tg_s, unit_s):
    t = TAPS[i]
    rhs = act[:, 0:ROWS] if t == 2 else xt[t - t // 3]
    tg_s[i % 2] = dot_nt(cot_v[...], rhs)
    for d in range(16):
        for ct in range(4):
            piece = tg_s[i % 2, 38 * d : 38 * d + 38, ct * 128 : (ct + 1) * 128]
            unit_s[d, 152 * i + 38 * ct : 152 * i + 38 * ct + 38, :] = piece


def resp_chunk(n, w5, act, xt, resp_v):
    cols = span(n)
    taps = jnp.concatenate([w5[t] for t in range(K2)], axis=1)
    rhs = jnp.concatenate([act[:, cols] if t == 2 else xt[t - t // 3, :, cols] for t in range(K2)], axis=0)
    resp_v[:, cols] = dot(taps, rhs).astype(BF16)


ORDER = ((0, 1, 2), (1, 2, 0), (2, 0, 1))
MESH = pl.DeviceIdType.MESH


def device_at(x, y, z, core):
    return ((y // 2) * 8 + z * 2 + core, (y % 2) * 4 + x)


def send(src, dst, ssem, rsem, to):
    return pltpu.make_async_remote_copy(
        src_ref=src, dst_ref=dst, send_sem=ssem, recv_sem=rsem, device_id=to, device_id_type=MESH
    )


def greet(me):
    barrier = pltpu.get_barrier_semaphore()
    x, y, z, core = me
    peers = []
    for dx in range(4):
        for dy in range(4):
            for dz in range(4):
                if (dx, dy, dz) != (0, 0, 0) and 0 in (dx, dy, dz):
                    peers.append(device_at((x + dx) % 4, (y + dy) % 4, (z + dz) % 4, core))
    for dz in range(4):
        peers.append(device_at(x, y, (z + dz) % 4, 1 - core))
    for peer in peers:
        pl.semaphore_signal(barrier, inc=1, device_id=peer, device_id_type=MESH)
    pl.semaphore_wait(barrier, len(peers))


def word_copies(dp, seq, packed, words, ws, wr):
    return [
        send(packed, words.at[seq], ws.at[d - 1], wr.at[d - 1], (dp, (seq + d) % SEQ)) for d in range(1, SEQ)
    ]


def rim_copies(dp, seq, pk, halo, hs, hr):
    return [
        send(pk.at[0], halo.at[1], hs.at[0], hr.at[0], (dp, (seq + SEQ - 1) % SEQ)),
        send(pk.at[1], halo.at[0], hs.at[1], hr.at[1], (dp, (seq + 1) % SEQ)),
    ]


def pack_group(g, me, unit_s, own, oth):
    core = me[3]
    for p in range(3):
        for j in range(64):
            at = [0, 0, 0]
            at[ORDER[p][0]], at[ORDER[p][1]], at[ORDER[p][2]] = j // 16, (j // 4) % 4, j % 4
            x, y, z = at
            unit = (y // 2) * 8 + z * 2
            r0 = g * 384 + p * 128 + x * 32 + (y % 2) * 16
            own[3 * g + p, j] = unit_s[unit + core, r0 : r0 + 16, :].astype(BF16)
            oth[3 * g + p, j] = unit_s[unit + 1 - core, r0 : r0 + 16, :].astype(BF16)


def pair_copy(g, me, oth, recv_d, ss, rs):
    x, y, z, core = me
    part = pl.ds(3 * g, 3)
    return send(oth.at[part], recv_d.at[part], ss.at[g], rs.at[g], device_at(x, y, z, 1 - core))


def pair_sum(g, own, recv_d):
    for p in range(3 * g, 3 * g + 3):
        for j in range(0, 64, 8):
            own[p, j : j + 8] = own[p, j : j + 8] + recv_d[p, j : j + 8]


def ring_copies(p, me, own, recv_1, ss, rs):
    axis = ORDER[p % 3][0]
    out = []
    for d in range(1, 4):
        to = list(me)
        to[axis] = (me[axis] + d) % 4
        src = own.at[p, pl.ds(to[axis] * 16, 16)]
        out.append(send(src, recv_1.at[p, d - 1], ss.at[p, d - 1], rs.at[p, d - 1], device_at(*to)))
    return out


def ring_sum(p, me, own, recv_1, buf_2):
    base = me[ORDER[p % 3][0]] * 16
    for j in range(16):
        total = own[p, base + j].astype(F32)
        for d in range(3):
            total = total + recv_1[p, d, j].astype(F32)
        buf_2[p, j] = total.astype(BF16)


def plane_copies(p, me, buf_2, recv_2, ss, rs):
    b, c = ORDER[p % 3][1], ORDER[p % 3][2]
    out = []
    for e in range(1, 16):
        to = list(me)
        to[b] = (me[b] + e // 4) % 4
        to[c] = (me[c] + e % 4) % 4
        src = buf_2.at[p, to[b] * 4 + to[c]]
        out.append(send(src, recv_2.at[p, e - 1], ss.at[p, e - 1], rs.at[p, e - 1], device_at(*to)))
    return out


def plane_sum(p, me, buf_2, recv_2, fin):
    total = buf_2[p, me[ORDER[p % 3][1]] * 4 + me[ORDER[p % 3][2]]].astype(F32)
    for e in range(15):
        total = total + recv_2[p, e].astype(F32)
    fin[p] = total.astype(BF16)


def share_copies(dp, seq, fin, gath, ss, rs):
    return [
        send(fin, gath.at[seq], ss.at[d - 1], rs.at[d - 1], (dp, (seq + d) % SEQ)) for d in range(1, SEQ)
    ]


def place_tower(gath, flat, tower_ref):
    for s in range(SEQ):
        for p in range(6):
            r0 = p * 128 + (s % 4) * 32 + (s // 4) * 16
            flat[r0 : r0 + 16, :] = gath[s, p].astype(F32)
    for i, t in enumerate(TAPS):
        for ct in range(4):
            j = 4 * i + ct
            tower_ref[t, :, ct * 128 : (ct + 1) * 128] = flat[38 * j : 38 * j + 38, :]


def pack_stem(stem_acc, gain_acc, gain, stb):
    even = stem_acc[0:C1, :]
    odd = jnp.concatenate([stem_acc[C1:, 4:64], stem_acc[C1:, 0:4]], axis=1)
    lane = lax.broadcasted_iota(I32, (C1, 64), 1)
    total = jnp.sum(gain_acc[...], axis=1, keepdims=True)
    both = jnp.where(lane < 60, even + odd, jnp.where(lane == 60, total, 0.0)).T
    row = lax.broadcasted_iota(I32, (8, 1), 0)
    last = jnp.where(row == 4, both[56:64] * (4.0 / gain[...]), both[56:64])
    for i in range(16):
        cols = slice((i // 8) * 256, (i // 8) * 256 + 256)
        stb[i] = last[:, cols] if i % 8 == 7 else both[(i % 8) * 8 : (i % 8) * 8 + 8, cols]


def stem_plane_copies(me, src_of, recv, slot_of, ss, rs):
    x, y, z, core = me
    out = []
    for e in range(1, 16):
        tx, ty = (x + e // 4) % 4, (y + e % 4) % 4
        out.append(
            send(src_of(tx * 4 + ty), recv.at[slot_of(e)], ss.at[e - 1], rs.at[e - 1], device_at(tx, ty, z, core))
        )
    return out


def stem_line_copies(me, piece, recv, ss, rs):
    x, y, z, core = me
    out = []
    for e in range(1, 8):
        to = device_at(x, y, (z + e // 2) % 4, (core + e % 2) % 2)
        out.append(send(piece, recv.at[z * 2 + core], ss.at[e - 1], rs.at[e - 1], to))
    return out


def place_stem(gath, stem_ref, gain_ref):
    for half in range(2):
        cols = slice(half * 256, half * 256 + 256)
        for s in range(K1):
            r = 4 * s
            stem_ref[s, :, cols] = gath[half * 8 + r // 8, r % 8 : r % 8 + 4, :]
        gain_ref[:, cols] = gath[half * 8 + 7, 4:5, :]


def start(copies):
    for c in copies:
        c.start()


def wait(copies):
    for c in copies:
        c.wait()


def whole_kernel(
    packed, rc_ref, sh_ref, cot_hbm, sw_ref, gain, w_hbm,
    resp_hbm, stem_ref, gain_ref, tower_ref,
    cot_v, w5, sw_f, wcat, gain_b, wt, gt, oh, act, xt,
    stem_s, ag, fac, sg_s, gain_acc, stem_acc, tg_s, unit_s,
    words, edge, pk, halo, rim, own, oth, recv_d, recv_1, buf_2, recv_2, fin, gath, flat,
    stb, recv_a, piece_a, recv_b, piece_b, gath_a,
    sems, ws, wr, hs, hr, ds, dr, s1, r1, s2, r2, s3, r3, sa, ra, sb, rb, sg, rg,
):
    dp, seq = lax.axis_index("dp"), lax.axis_index("seq")
    x, y, z, core = seq % 4, (dp // 8) * 2 + seq // 4, (dp // 2) % 4, dp % 2
    me = (x, y, z, core)
    ends = [
        pltpu.make_async_copy(cot_hbm.at[:, 0:128], edge.at[0], sems.at[9]),
        pltpu.make_async_copy(cot_hbm.at[:, ROWS - 128 : ROWS], edge.at[1], sems.at[10]),
    ]
    cuts = (0, 160, 320, 464, F2)
    cots = [
        pltpu.make_async_copy(
            cot_hbm.at[cuts[i] : cuts[i + 1], :], cot_v.at[cuts[i] : cuts[i + 1], :], sems.at[i]
        )
        for i in range(4)
    ]
    weights = [pltpu.make_async_copy(w_hbm.at[t], w5.at[t], sems.at[4 + t]) for t in range(K2)]
    start(ends)
    start(cots)
    start(weights)
    greet(me)
    edges = word_copies(dp, seq, packed, words, ws, wr)
    start(edges)
    for i in range(2):
        ends[i].wait()
        pk[i] = edge[i].T[0:16] if i == 0 else edge[i].T[112:128]
    rims = rim_copies(dp, seq, pk, halo, hs, hr)
    start(rims)
    words[seq] = packed[...]
    gain_acc[...] = jnp.zeros_like(gain_acc)
    stem_acc[...] = jnp.zeros_like(stem_acc)
    unit_s[:, 760:768, :] = jnp.zeros((16, 8, 128), F32)
    prep_stem_weight(sw_ref, sw_f, wcat, gain, gain_b)
    wait(cots)
    prep_cot(cot_v, gt)
    wait(weights)
    prep_tower_weight(w5, wt)
    for n in range(1, 4):
        ag_chunk(n, wt, gt, ag)
    wait(edges)
    decode(words, rc_ref[0], sh_ref[0], seq, oh)
    for n in range(8):
        stem_chunk(n, wcat, oh, stem_s)
        act_chunk(n, seq, stem_s, gain_b, act)

    def tap(i):
        if i != 0:
            shift_act(TAPS[i], act, xt)
        tower_tap(i, cot_v, act, xt, tg_s, unit_s)

    pairs, rings, planes = [], [], []

    def pair(g):
        pack_group(g, me, unit_s, own, oth)
        pairs.append(pair_copy(g, me, oth, recv_d, ds, dr))
        pairs[g].start()

    def ring(g):
        pairs[g].wait()
        pair_sum(g, own, recv_d)
        for p in range(3 * g, 3 * g + 3):
            rings.append(ring_copies(p, me, own, recv_1, s1, r1))
            start(rings[p])

    def plane(g):
        for p in range(3 * g, 3 * g + 3):
            wait(rings[p])
            ring_sum(p, me, own, recv_1, buf_2)
            planes.append(plane_copies(p, me, buf_2, recv_2, s2, r2))
            start(planes[p])

    def factor(*chunks):
        for n in chunks:
            stem_chunk(n, wcat, oh, stem_s)
            factor_chunk(n, stem_s, gain_b, fac)

    def resp(n):
        resp_chunk(n, w5, act, xt, cot_v)

    tap(0)
    factor(0)
    tap(1)
    factor(1, 2)
    tap(2)
    pair(0)
    factor(3, 4)
    tap(3)
    ring(0)
    factor(5, 6)
    tap(4)
    pair(1)
    factor(7)
    wait(rims)
    rim_cot(cot_v, halo, seq, rim, gt)
    ag_chunk(4, wt, gt, ag)
    ring(1)
    for n in (5, 6, 0, 7):
        ag_chunk(n, wt, gt, ag)
    for n in range(8):
        back_chunk(n, ag, fac, sg_s, gain_acc)
        stem_grad_chunk(n, sg_s, oh, stem_acc)
    pack_stem(stem_acc, gain_acc, gain, stb)
    level_a = stem_plane_copies(me, lambda a: stb.at[a], recv_a, lambda e: e - 1, sa, ra)
    start(level_a)
    plane(0)
    resp(0)
    resp(1)
    resp(2)
    plane(1)
    resp(3)
    resp(4)
    wait(level_a)
    total = stb[x * 4 + y]
    for e in range(15):
        total = total + recv_a[e]
    piece_a[...] = total
    recv_b[z * 2 + core] = total
    level_b = stem_line_copies(me, piece_a, recv_b, sb, rb)
    start(level_b)
    resp(5)
    resp(6)
    resp(7)
    c3 = pltpu.make_async_copy(cot_v, resp_hbm, sems.at[0])
    c3.start()
    for p in range(6):
        wait(planes[p])
        plane_sum(p, me, buf_2, recv_2, fin)
    share = share_copies(dp, seq, fin, gath, s3, r3)
    start(share)
    gath[seq] = fin[...]
    wait(level_b)
    total = recv_b[0]
    for e in range(1, 8):
        total = total + recv_b[e]
    piece_b[...] = total
    gath_a[x * 4 + y] = total
    level_c = stem_plane_copies(me, lambda a: piece_b, gath_a, lambda e: x * 4 + y, sg, rg)
    start(level_c)
    c3.wait()
    wait(share)
    place_tower(gath, flat, tower_ref)
    wait(level_c)
    place_stem(gath_a, stem_ref, gain_ref)


def scratch():
    V = pltpu.VMEM
    D = pltpu.SemaphoreType.DMA
    return [
        V((F2, ROWS), BF16),
        V((K2, F2, C1), BF16),
        V((128, C1), F32),
        V((2 * C1, 128), BF16),
        V((C1, 128), F32),
        V((C1, KF), BF16),
        V((KF, ROWS), BF16),
        V((128, WIDE), BF16),
        V((C1, WIDE), BF16),
        V((K2 - 1, C1, ROWS), BF16),
        V((2, 2 * C1, CH), F32),
        V((C1, ROWS), BF16),
        V((3, C1, ROWS), BF16),
        V((2, 2 * C1, CH), BF16),
        V((C1, 128), F32),
        V((2 * C1, 64), F32),
        V((2, F2, C1), F32),
        V((16, UNIT, 128), F32),
        V((SEQ, 1, 256), I32),
        V((2, F2, 128), BF16),
        V((2, 16, F2), BF16),
        V((2, 16, F2), BF16),
        V((F2, 128), BF16),
        V((6, 64, 16, 128), BF16),
        V((6, 64, 16, 128), BF16),
        V((6, 64, 16, 128), BF16),
        V((6, 3, 16, 16, 128), BF16),
        V((6, 16, 16, 128), BF16),
        V((6, 15, 16, 128), BF16),
        V((6, 16, 128), BF16),
        V((SEQ, 6, 16, 128), BF16),
        V((UNIT, 128), F32),
        V((16, 8, 256), F32),
        V((15, 8, 256), F32),
        V((8, 256), F32),
        V((8, 8, 256), F32),
        V((8, 256), F32),
        V((16, 8, 256), F32),
        D((11,)), D((7,)), D((7,)), D((2,)), D((2,)), D((2,)), D((2,)),
        D((6, 3)), D((6, 3)), D((6, 15)), D((6, 15)), D((7,)), D((7,)),
        D((15,)), D((15,)), D((7,)), D((7,)), D((15,)), D((15,)),
    ]


CUTS = (0, 80, 160, 240, 320, 400, 480, 544, F2)


def hand_over(resp, stem, gain, tower, resp_o, stem_o, gain_o, tower_o, resp_v, stem_v, gain_v, tower_v, si, so):
    way = [(stem, stem_v, stem_o), (gain, gain_v, gain_o), (tower, tower_v, tower_o)]
    for i in range(8):
        rows = slice(CUTS[i], CUTS[i + 1])
        way.append((resp.at[rows, :], resp_v.at[rows, :], resp_o.at[rows, :]))
    into = [pltpu.make_async_copy(w[0], w[1], si.at[i]) for i, w in enumerate(way)]
    out = [pltpu.make_async_copy(w[1], w[2], so.at[i]) for i, w in enumerate(way)]
    start(into)
    for i in range(len(way)):
        into[i].wait()
        out[i].start()
    wait(out)


def shards(packed, rc_flags, shifts, cotangent, stem_weight, pool_gain, tower_weight):
    S = pl.BlockSpec(memory_space=pltpu.SMEM)
    VM = pl.BlockSpec(memory_space=pltpu.VMEM)
    A = pl.BlockSpec(memory_space=pl.ANY)
    resp, stem, gain, tower = pl.pallas_call(
        whole_kernel,
        out_shape=(
            jax.ShapeDtypeStruct((F2, ROWS), BF16),
            jax.ShapeDtypeStruct((K1, 4, C1), F32),
            jax.ShapeDtypeStruct((1, C1), F32),
            jax.ShapeDtypeStruct((K2, 38, C1), F32),
        ),
        in_specs=[VM, S, S, A, VM, VM, A],
        out_specs=(A, VM, VM, VM),
        scratch_shapes=scratch(),
        compiler_params=pltpu.CompilerParams(
            vmem_limit_bytes=62 * 1024 * 1024, collective_id=0, has_side_effects=True
        ),
    )(
        packed, rc_flags, shifts, cotangent[0].T, stem_weight, pool_gain[None],
        jnp.transpose(tower_weight, (1, 0, 2)),
    )
    resp, stem, gain, tower = pl.pallas_call(
        hand_over,
        out_shape=tuple(jax.ShapeDtypeStruct(v.shape, v.dtype) for v in (resp, stem, gain, tower)),
        in_specs=[A] * 4,
        out_specs=(A,) * 4,
        scratch_shapes=[
            pltpu.VMEM((F2, ROWS), BF16),
            pltpu.VMEM((K1, 4, C1), F32),
            pltpu.VMEM((1, C1), F32),
            pltpu.VMEM((K2, 38, C1), F32),
            pltpu.SemaphoreType.DMA((11,)),
            pltpu.SemaphoreType.DMA((11,)),
        ],
        compiler_params=pltpu.CompilerParams(vmem_limit_bytes=60 * 1024 * 1024),
    )(resp, stem, gain, tower)
    return resp.T[None], stem, gain[0], jnp.transpose(tower, (1, 0, 2))


def solution(mesh):
    in_specs = (P("dp", "seq"), P("dp"), P("dp"), P("dp", "seq", None), P(), P(), P())
    out_specs = (P("dp", "seq", None), P(), P(), P("dp", None, None))
    return jax.shard_map(shards, mesh=mesh, in_specs=in_specs, out_specs=out_specs, check_vma=False)
```

```python
import functools
import jax
import jax.numpy as jnp
from jax import lax
from jax.experimental import pallas as pl
from jax.experimental.pallas import tpu as pltpu
from jax.sharding import PartitionSpec as P

F32, BF16, I32 = jnp.float32, jnp.bfloat16, jnp.int32
C1, F2, K1, K2 = 512, 608, 15, 5
ROWS = 1920
WIDE = 2048
KF = 3072
UNIT = 768
SEQ = 8
CH = 256


def dot(a, b):
    return lax.dot_general(a, b, (((1,), (0,)), ((), ())), preferred_element_type=F32)


def dot_nt(a, b):
    return lax.dot_general(a, b, (((1,), (1,)), ((), ())), preferred_element_type=F32)


def prep_stem_weight(sw_ref, sw_f, wcat, gain, gain_b):
    sw_f[60:68, :] = jnp.zeros((8, C1), F32)
    for s in range(K1):
        v = sw_ref[s].astype(F32) * 0.25
        sw_f[4 * s : 4 * s + 4, :] = v
        sw_f[68 + 4 * s : 72 + 4 * s, :] = v
    w = sw_f[...].T
    lane = lax.broadcasted_iota(I32, (C1, 128), 1)
    wcat[0:C1, :] = jnp.where(lane < 64, w, -w).astype(BF16)
    wcat[C1:, :] = w.astype(BF16)
    gain_b[...] = jnp.broadcast_to(gain[...], (128, C1)).T * 2.0


def prep_tower_weight(w5, wt):
    flat = w5.reshape(K2 * F2, C1)

    def block(i, _):
        r0 = pl.multiple_of(i * 128, 128)
        wt[:, pl.ds(r0, 128)] = flat[pl.ds(r0, 128), :].T
        return 0

    lax.fori_loop(0, (K2 * F2) // 128, block, 0, unroll=True)
    tail = K2 * F2 - (K2 * F2) // 128 * 128
    v = jnp.concatenate([flat[K2 * F2 - tail :, :], jnp.zeros((128 - tail, C1), BF16)], axis=0)
    wt[:, KF - 128 :] = v.T


def prep_cot(cot_v, gt):
    def rows(i, _):
        r0 = pl.multiple_of(i * 16, 16)
        full = cot_v[pl.ds(r0, 16), :]
        for t in range(K2):
            s = 2 - t
            v = full if s == 0 else pltpu.roll(full, (-s) % ROWS, 1)
            gt[pl.ds(pl.multiple_of(t * F2 + r0, 16), 16), :] = v
        return 0

    lax.fori_loop(0, F2 // 16, rows, 0, unroll=True)
    gt[K2 * F2 : KF, :] = jnp.zeros((KF - K2 * F2, ROWS), BF16)


def rim_cot(cot_v, halo, seq, rim, gt):
    nxt = jnp.where(seq < SEQ - 1, halo[1].astype(F32), 0.0)
    prv = jnp.where(seq > 0, halo[0].astype(F32), 0.0)
    rim[...] = jnp.concatenate([nxt, jnp.zeros((96, F2), F32), prv], axis=0).T.astype(BF16)
    for r in range(0, F2, 16):
        rs = slice(r, r + 16)
        ring = jnp.concatenate([cot_v[rs, ROWS - 256 : ROWS], rim[rs, :], cot_v[rs, 0:256]], axis=1)
        for t in range(K2):
            s = 2 - t
            if s != 0:
                v = pltpu.roll(ring, (-s) % 640, 1)
                gt[t * F2 + r : t * F2 + r + 16, ROWS - 128 : ROWS] = v[:, 128:256]
                gt[t * F2 + r : t * F2 + r + 16, 0:128] = v[:, 384:512]


def decode(words, rc, shift, seq, oh):
    take = jnp.where(rc == 1, SEQ - 1 - seq, seq)
    slot = lax.broadcasted_iota(I32, (SEQ, 1, CH), 0)
    w8 = words[...]
    own = jnp.sum(jnp.where(slot == take, w8, 0), axis=0)
    low = jnp.sum(jnp.where(slot == take - 1, w8, 0), axis=0)
    high = jnp.sum(jnp.where(slot == take + 1, w8, 0), axis=0)
    lane = lax.broadcasted_iota(I32, (1, 128), 1)
    rim = jnp.where(lane == 127, low[:, 128:256], jnp.where(lane == 0, high[:, 0:128], 0))
    row = jnp.broadcast_to(jnp.concatenate([own, rim], axis=1), (8, 384))
    after = jnp.where(rc == 1, pltpu.roll(row, 1, 1), pltpu.roll(row, 383, 1))
    sub = lax.broadcasted_iota(I32, (8, 384), 0)
    planes = (jnp.where(sub < 4, row, after) >> (8 * (sub & 3))) & 255
    planes = planes.astype(F32).astype(BF16)
    src = lax.broadcasted_iota(I32, (384, CH), 0)
    src = jnp.where(src == 383, -1, src)
    part = lax.broadcasted_iota(I32, (64, CH), 0)
    s = part >> 2
    want = jnp.where(rc == 1, 3 - (part & 3), part & 3)

    def chunk(i, _):
        u0 = pl.multiple_of(i * CH, CH)
        u = u0 + lax.broadcasted_iota(I32, (1, CH), 1)
        q = jnp.where(u < 1984, u, u - WIDE)
        b0 = 2 * q - 7 - shift
        j0 = (((b0 + 30) * 34953) >> 19) - 2
        i0 = b0 - 15 * j0
        at = jnp.where(rc == 1, 255 - j0, j0)
        sel = jnp.where(src == at, 1.0, 0.0).astype(BF16)
        got = dot(planes, sel).astype(I32)
        word_a = got[0:1] + (got[1:2] << 8) + (got[2:3] << 16) + (got[3:4] << 24)
        word_b = got[4:5] + (got[5:6] << 8) + (got[6:7] << 16) + (got[7:8] << 24)
        d = i0 + s
        late = d >= 15
        word = jnp.where(late, word_b, word_a)
        d = jnp.where(late, d - 15, d)
        d = jnp.where(rc == 1, 14 - d, d)
        where = 2 * ROWS * seq + b0 + s
        good = (where >= 0) & (where < 2 * ROWS * SEQ)
        hit = (((word >> (2 * d)) & 3) == want) & good
        hot = jnp.where(hit, 1.0, 0.0).astype(BF16)
        oh[0:64, pl.ds(u0, CH)] = hot
        oh[64:128, pl.ds(u0, CH)] = hot
        return 0

    lax.fori_loop(0, WIDE // CH, chunk, 0, unroll=True)


GELU_A = 0.7978845608028654
GELU_B = 0.044715


def activate(hd, mean, gain2):
    hx = mean + jnp.tanh(gain2 * hd) * hd
    th = jnp.tanh(hx * (2 * GELU_A + (8 * GELU_A * GELU_B) * (hx * hx)))
    return hx * (1.0 + th)


def factors(hd, mean, gain2):
    gd = gain2 * hd
    t = jnp.tanh(gd)
    hx = mean + t * hd
    h2 = hx * hx
    p1 = 1.0 + jnp.tanh(hx * (2 * GELU_A + (8 * GELU_A * GELU_B) * h2))
    dgelu = p1 * (0.25 + hx * (2.0 - p1) * (0.5 * GELU_A + (6 * GELU_A * GELU_B) * h2))
    k = gd * (1.0 - t * t)
    m1 = (1.0 + t) + k
    return dgelu * m1, dgelu * (2.0 - m1), dgelu * (hd * k)


def span(n):
    return slice(n * CH, min((n + 1) * CH, ROWS))


def ag_chunk(n, wt, gt, ag):
    ag[:, span(n)] = dot(wt[...], gt[:, span(n)]).astype(BF16)


def stem_chunk(n, wcat, oh, stem_s):
    stem_s[n % 2] = dot(wcat[...], oh[:, n * CH : (n + 1) * CH])


def act_chunk(n, seq, stem_s, gain_b, act):
    for r in range(0, C1, 16):
        for lt in range(2):
            cols = slice(lt * 128, lt * 128 + 128)
            at = slice(n * CH + lt * 128, n * CH + lt * 128 + 128)
            a = activate(
                stem_s[n % 2, r : r + 16, cols], stem_s[n % 2, C1 + r : C1 + r + 16, cols], gain_b[r : r + 16, :]
            )
            if at.start >= ROWS:
                lane = lax.broadcasted_iota(I32, (16, 128), 1)
                out = ((lane < 64) & (seq == SEQ - 1)) | ((lane >= 64) & (seq == 0))
                a = jnp.where(out, 0.0, a)
            act[r : r + 16, at] = a.astype(BF16)


def factor_chunk(n, stem_s, gain_b, fac):
    for r in range(0, C1, 16):
        for c0 in range(span(n).start, span(n).stop, 128):
            cols = slice(c0 % CH, c0 % CH + 128)
            made = factors(
                stem_s[n % 2, r : r + 16, cols], stem_s[n % 2, C1 + r : C1 + r + 16, cols], gain_b[r : r + 16, :]
            )
            for i in range(3):
                fac[i, r : r + 16, c0 : c0 + 128] = made[i].astype(BF16)


def back_chunk(n, ag, fac, sg_s, gain_acc):
    for r in range(0, C1, 16):
        for c0 in range(span(n).start, span(n).stop, 128):
            rs, cs = slice(r, r + 16), slice(c0, c0 + 128)
            o = slice(c0 % CH, c0 % CH + 128)
            g = ag[rs, cs]
            sg_s[n % 2, rs, o] = g * fac[0, rs, cs]
            sg_s[n % 2, C1 + r : C1 + r + 16, o] = g * fac[1, rs, cs]
            gain_acc[rs, :] += g.astype(F32) * fac[2, rs, cs].astype(F32)


def stem_grad_chunk(n, sg_s, oh, stem_acc):
    w = span(n).stop - span(n).start
    stem_acc[...] += dot_nt(sg_s[n % 2, :, 0:w], oh[0:64, span(n)])


def shift_act(t, act, xt):
    s = t - 2
    for r in range(0, C1, 16):
        v = pltpu.roll(act[r : r + 16, :], (-s) % WIDE, 1)
        xt[t - t // 3, r : r + 16, :] = v[:, 0:ROWS]


TAPS = (2, 1, 3, 0, 4)


def tower_tap(i, cot_v, act, xt, tg_s, unit_s):
    t = TAPS[i]
    rhs = act[:, 0:ROWS] if t == 2 else xt[t - t // 3]
    tg_s[i % 2] = dot_nt(cot_v[...], rhs)
    for d in range(16):
        for ct in range(4):
            piece = tg_s[i % 2, 38 * d : 38 * d + 38, ct * 128 : (ct + 1) * 128]
            unit_s[d, 152 * i + 38 * ct : 152 * i + 38 * ct + 38, :] = piece


def resp_chunk(n, w5, act, xt, resp_v):
    cols = span(n)
    taps = jnp.concatenate([w5[t] for t in range(K2)], axis=1)
    rhs = jnp.concatenate([act[:, cols] if t == 2 else xt[t - t // 3, :, cols] for t in range(K2)], axis=0)
    resp_v[:, cols] = dot(taps, rhs).astype(BF16)


ORDER = ((0, 1, 2), (1, 2, 0), (2, 0, 1))
MESH = pl.DeviceIdType.MESH


def device_at(x, y, z, core):
    return ((y // 2) * 8 + z * 2 + core, (y % 2) * 4 + x)


def send(src, dst, ssem, rsem, to):
    return pltpu.make_async_remote_copy(
        src_ref=src, dst_ref=dst, send_sem=ssem, recv_sem=rsem, device_id=to, device_id_type=MESH
    )


def greet(me):
    barrier = pltpu.get_barrier_semaphore()
    x, y, z, core = me
    peers = []
    for dx in range(4):
        for dy in range(4):
            for dz in range(4):
                if (dx, dy, dz) != (0, 0, 0) and 0 in (dx, dy, dz):
                    peers.append(device_at((x + dx) % 4, (y + dy) % 4, (z + dz) % 4, core))
    for dz in range(4):
        peers.append(device_at(x, y, (z + dz) % 4, 1 - core))
    for peer in peers:
        pl.semaphore_signal(barrier, inc=1, device_id=peer, device_id_type=MESH)
    pl.semaphore_wait(barrier, len(peers))


def word_copies(dp, seq, packed, words, ws, wr):
    return [
        send(packed, words.at[seq], ws.at[d - 1], wr.at[d - 1], (dp, (seq + d) % SEQ)) for d in range(1, SEQ)
    ]


def rim_copies(dp, seq, pk, halo, hs, hr):
    return [
        send(pk.at[0], halo.at[1], hs.at[0], hr.at[0], (dp, (seq + SEQ - 1) % SEQ)),
        send(pk.at[1], halo.at[0], hs.at[1], hr.at[1], (dp, (seq + 1) % SEQ)),
    ]


def pack_group(g, me, unit_s, own, oth):
    core = me[3]
    for p in range(3):
        for j in range(64):
            at = [0, 0, 0]
            at[ORDER[p][0]], at[ORDER[p][1]], at[ORDER[p][2]] = j // 16, (j // 4) % 4, j % 4
            x, y, z = at
            unit = (y // 2) * 8 + z * 2
            r0 = g * 384 + p * 128 + x * 32 + (y % 2) * 16
            own[3 * g + p, j] = unit_s[unit + core, r0 : r0 + 16, :].astype(BF16)
            oth[3 * g + p, j] = unit_s[unit + 1 - core, r0 : r0 + 16, :].astype(BF16)


def pair_copy(g, me, oth, recv_d, ss, rs):
    x, y, z, core = me
    part = pl.ds(3 * g, 3)
    return send(oth.at[part], recv_d.at[part], ss.at[g], rs.at[g], device_at(x, y, z, 1 - core))


def pair_sum(g, own, recv_d):
    for p in range(3 * g, 3 * g + 3):
        for j in range(0, 64, 8):
            own[p, j : j + 8] = own[p, j : j + 8] + recv_d[p, j : j + 8]


def ring_copies(p, me, own, recv_1, ss, rs):
    axis = ORDER[p % 3][0]
    out = []
    for d in range(1, 4):
        to = list(me)
        to[axis] = (me[axis] + d) % 4
        src = own.at[p, pl.ds(to[axis] * 16, 16)]
        out.append(send(src, recv_1.at[p, d - 1], ss.at[p, d - 1], rs.at[p, d - 1], device_at(*to)))
    return out


def ring_sum(p, me, own, recv_1, buf_2):
    base = me[ORDER[p % 3][0]] * 16
    for j in range(16):
        total = own[p, base + j].astype(F32)
        for d in range(3):
            total = total + recv_1[p, d, j].astype(F32)
        buf_2[p % 3, j, p // 3] = total.astype(BF16)


def plane_copies(p, me, buf_2, recv_2, ss, rs):
    b, c = ORDER[p % 3][1], ORDER[p % 3][2]
    out = []
    for e in range(1, 16):
        to = list(me)
        to[b] = (me[b] + e // 4) % 4
        to[c] = (me[c] + e % 4) % 4
        src = buf_2.at[p, to[b] * 4 + to[c]]
        out.append(send(src, recv_2.at[p, e - 1], ss.at[p, e - 1], rs.at[p, e - 1], device_at(*to)))
    return out


def plane_sum(p, me, buf_2, recv_2, fin):
    total = buf_2[p, me[ORDER[p][1]] * 4 + me[ORDER[p][2]]].astype(F32)
    for e in range(15):
        total = total + recv_2[p, e].astype(F32)
    for g in range(2):
        fin[3 * g + p] = total[g].astype(BF16)


def share_copies(dp, seq, fin, gath, ss, rs):
    return [
        send(fin, gath.at[seq], ss.at[d - 1], rs.at[d - 1], (dp, (seq + d) % SEQ)) for d in range(1, SEQ)
    ]


def place_tower(gath, flat, tower_ref):
    for s in range(SEQ):
        for p in range(6):
            r0 = p * 128 + (s % 4) * 32 + (s // 4) * 16
            flat[r0 : r0 + 16, :] = gath[s, p].astype(F32)
    for i, t in enumerate(TAPS):
        for ct in range(4):
            j = 4 * i + ct
            tower_ref[t, :, ct * 128 : (ct + 1) * 128] = flat[38 * j : 38 * j + 38, :]


def pack_stem(stem_acc, gain_acc, gain, stb):
    even = stem_acc[0:C1, :]
    odd = jnp.concatenate([stem_acc[C1:, 4:64], stem_acc[C1:, 0:4]], axis=1)
    lane = lax.broadcasted_iota(I32, (C1, 64), 1)
    total = jnp.sum(gain_acc[...], axis=1, keepdims=True)
    both = jnp.where(lane < 60, even + odd, jnp.where(lane == 60, total, 0.0)).T
    row = lax.broadcasted_iota(I32, (8, 1), 0)
    last = jnp.where(row == 4, both[56:64] * (4.0 / gain[...]), both[56:64])
    for i in range(16):
        cols = slice((i // 8) * 256, (i // 8) * 256 + 256)
        stb[i] = last[:, cols] if i % 8 == 7 else both[(i % 8) * 8 : (i % 8) * 8 + 8, cols]


def stem_plane_copies(me, src_of, recv, slot_of, ss, rs):
    x, y, z, core = me
    out = []
    for e in range(1, 16):
        tx, ty = (x + e // 4) % 4, (y + e % 4) % 4
        out.append(
            send(src_of(tx * 4 + ty), recv.at[slot_of(e)], ss.at[e - 1], rs.at[e - 1], device_at(tx, ty, z, core))
        )
    return out


def stem_line_copies(me, piece, recv, ss, rs):
    x, y, z, core = me
    out = []
    for e in range(1, 8):
        to = device_at(x, y, (z + e // 2) % 4, (core + e % 2) % 2)
        out.append(send(piece, recv.at[z * 2 + core], ss.at[e - 1], rs.at[e - 1], to))
    return out


def place_stem(gath, stem_ref, gain_ref):
    for half in range(2):
        cols = slice(half * 256, half * 256 + 256)
        for s in range(K1):
            r = 4 * s
            stem_ref[s, :, cols] = gath[half * 8 + r // 8, r % 8 : r % 8 + 4, :]
        gain_ref[:, cols] = gath[half * 8 + 7, 4:5, :]


def start(copies):
    for c in copies:
        c.start()


def wait(copies):
    for c in copies:
        c.wait()


def whole_kernel(
    packed, rc_ref, sh_ref, cot_hbm, sw_ref, gain, w_hbm,
    resp_hbm, stem_ref, gain_ref, tower_ref,
    cot_v, w5, sw_f, wcat, gain_b, wt, gt, oh, act, xt,
    stem_s, ag, fac, sg_s, gain_acc, stem_acc, tg_s, unit_s,
    words, edge, pk, halo, rim, own, oth, recv_d, recv_1, buf_2, recv_2, fin, gath, flat,
    stb, recv_a, piece_a, recv_b, piece_b, gath_a,
    sems, ws, wr, hs, hr, ds, dr, s1, r1, s2, r2, s3, r3, sa, ra, sb, rb, sg, rg,
):
    dp, seq = lax.axis_index("dp"), lax.axis_index("seq")
    x, y, z, core = seq % 4, (dp // 8) * 2 + seq // 4, (dp // 2) % 4, dp % 2
    me = (x, y, z, core)
    ends = [
        pltpu.make_async_copy(cot_hbm.at[:, 0:128], edge.at[0], sems.at[9]),
        pltpu.make_async_copy(cot_hbm.at[:, ROWS - 128 : ROWS], edge.at[1], sems.at[10]),
    ]
    cuts = (0, 160, 320, 464, F2)
    cots = [
        pltpu.make_async_copy(
            cot_hbm.at[cuts[i] : cuts[i + 1], :], cot_v.at[cuts[i] : cuts[i + 1], :], sems.at[i]
        )
        for i in range(4)
    ]
    weights = [pltpu.make_async_copy(w_hbm.at[t], w5.at[t], sems.at[4 + t]) for t in range(K2)]
    start(ends)
    start(cots)
    start(weights)
    greet(me)
    edges = word_copies(dp, seq, packed, words, ws, wr)
    start(edges)
    for i in range(2):
        ends[i].wait()
        pk[i] = edge[i].T[0:16] if i == 0 else edge[i].T[112:128]
    rims = rim_copies(dp, seq, pk, halo, hs, hr)
    start(rims)
    words[seq] = packed[...]
    gain_acc[...] = jnp.zeros_like(gain_acc)
    stem_acc[...] = jnp.zeros_like(stem_acc)
    unit_s[:, 760:768, :] = jnp.zeros((16, 8, 128), F32)
    prep_stem_weight(sw_ref, sw_f, wcat, gain, gain_b)
    wait(cots)
    prep_cot(cot_v, gt)
    wait(weights)
    prep_tower_weight(w5, wt)
    for n in range(1, 4):
        ag_chunk(n, wt, gt, ag)
    wait(edges)
    decode(words, rc_ref[0], sh_ref[0], seq, oh)
    for n in range(8):
        stem_chunk(n, wcat, oh, stem_s)
        act_chunk(n, seq, stem_s, gain_b, act)

    def tap(i):
        if i != 0:
            shift_act(TAPS[i], act, xt)
        tower_tap(i, cot_v, act, xt, tg_s, unit_s)

    pairs, rings, planes = [], [], []

    def pair(g):
        pack_group(g, me, unit_s, own, oth)
        pairs.append(pair_copy(g, me, oth, recv_d, ds, dr))
        pairs[g].start()

    def ring(g):
        pairs[g].wait()
        pair_sum(g, own, recv_d)
        for p in range(3 * g, 3 * g + 3):
            rings.append(ring_copies(p, me, own, recv_1, s1, r1))
            start(rings[p])

    def ring_end(g):
        for p in range(3 * g, 3 * g + 3):
            wait(rings[p])
            ring_sum(p, me, own, recv_1, buf_2)

    def plane(p):
        planes.append(plane_copies(p, me, buf_2, recv_2, s2, r2))
        start(planes[p])

    def factor(*chunks):
        for n in chunks:
            stem_chunk(n, wcat, oh, stem_s)
            factor_chunk(n, stem_s, gain_b, fac)

    def resp(n):
        resp_chunk(n, w5, act, xt, cot_v)

    tap(0)
    factor(0)
    tap(1)
    factor(1, 2)
    tap(2)
    pair(0)
    factor(3, 4)
    tap(3)
    ring(0)
    factor(5, 6)
    tap(4)
    pair(1)
    factor(7)
    wait(rims)
    rim_cot(cot_v, halo, seq, rim, gt)
    ag_chunk(4, wt, gt, ag)
    ring(1)
    for n in (5, 6, 0, 7):
        ag_chunk(n, wt, gt, ag)
    for n in range(8):
        back_chunk(n, ag, fac, sg_s, gain_acc)
        stem_grad_chunk(n, sg_s, oh, stem_acc)
    pack_stem(stem_acc, gain_acc, gain, stb)
    level_a = stem_plane_copies(me, lambda a: stb.at[a], recv_a, lambda e: e - 1, sa, ra)
    start(level_a)
    ring_end(0)
    resp(0)
    resp(1)
    resp(2)
    ring_end(1)
    for p in range(3):
        plane(p)
    wait(level_a)
    total = stb[x * 4 + y]
    for e in range(15):
        total = total + recv_a[e]
    piece_a[...] = total
    recv_b[z * 2 + core] = total
    level_b = stem_line_copies(me, piece_a, recv_b, sb, rb)
    start(level_b)
    resp(3)
    resp(4)
    resp(5)
    resp(6)
    for p in range(3):
        wait(planes[p])
        plane_sum(p, me, buf_2, recv_2, fin)
    share = share_copies(dp, seq, fin, gath, s3, r3)
    start(share)
    gath[seq] = fin[...]
    wait(level_b)
    total = recv_b[0]
    for e in range(1, 8):
        total = total + recv_b[e]
    piece_b[...] = total
    gath_a[x * 4 + y] = total
    level_c = stem_plane_copies(me, lambda a: piece_b, gath_a, lambda e: x * 4 + y, sg, rg)
    start(level_c)
    resp(7)
    c3 = pltpu.make_async_copy(cot_v, resp_hbm, sems.at[0])
    c3.start()
    c3.wait()
    wait(share)
    place_tower(gath, flat, tower_ref)
    wait(level_c)
    place_stem(gath_a, stem_ref, gain_ref)


def scratch():
    V = pltpu.VMEM
    D = pltpu.SemaphoreType.DMA
    return [
        V((F2, ROWS), BF16),
        V((K2, F2, C1), BF16),
        V((128, C1), F32),
        V((2 * C1, 128), BF16),
        V((C1, 128), F32),
        V((C1, KF), BF16),
        V((KF, ROWS), BF16),
        V((128, WIDE), BF16),
        V((C1, WIDE), BF16),
        V((K2 - 1, C1, ROWS), BF16),
        V((2, 2 * C1, CH), F32),
        V((C1, ROWS), BF16),
        V((3, C1, ROWS), BF16),
        V((2, 2 * C1, CH), BF16),
        V((C1, 128), F32),
        V((2 * C1, 64), F32),
        V((2, F2, C1), F32),
        V((16, UNIT, 128), F32),
        V((SEQ, 1, 256), I32),
        V((2, F2, 128), BF16),
        V((2, 16, F2), BF16),
        V((2, 16, F2), BF16),
        V((F2, 128), BF16),
        V((6, 64, 16, 128), BF16),
        V((6, 64, 16, 128), BF16),
        V((6, 64, 16, 128), BF16),
        V((6, 3, 16, 16, 128), BF16),
        V((3, 16, 2, 16, 128), BF16),
        V((3, 15, 2, 16, 128), BF16),
        V((6, 16, 128), BF16),
        V((SEQ, 6, 16, 128), BF16),
        V((UNIT, 128), F32),
        V((16, 8, 256), F32),
        V((15, 8, 256), F32),
        V((8, 256), F32),
        V((8, 8, 256), F32),
        V((8, 256), F32),
        V((16, 8, 256), F32),
        D((11,)), D((7,)), D((7,)), D((2,)), D((2,)), D((2,)), D((2,)),
        D((6, 3)), D((6, 3)), D((3, 15)), D((3, 15)), D((7,)), D((7,)),
        D((15,)), D((15,)), D((7,)), D((7,)), D((15,)), D((15,)),
    ]


CUTS = (0, 80, 160, 240, 320, 400, 480, 544, F2)


def hand_over(resp, stem, gain, tower, resp_o, stem_o, gain_o, tower_o, resp_v, stem_v, gain_v, tower_v, si, so):
    way = [(stem, stem_v, stem_o), (gain, gain_v, gain_o), (tower, tower_v, tower_o)]
    for i in range(8):
        rows = slice(CUTS[i], CUTS[i + 1])
        way.append((resp.at[rows, :], resp_v.at[rows, :], resp_o.at[rows, :]))
    into = [pltpu.make_async_copy(w[0], w[1], si.at[i]) for i, w in enumerate(way)]
    out = [pltpu.make_async_copy(w[1], w[2], so.at[i]) for i, w in enumerate(way)]
    start(into)
    for i in range(len(way)):
        into[i].wait()
        out[i].start()
    wait(out)


def shards(packed, rc_flags, shifts, cotangent, stem_weight, pool_gain, tower_weight):
    S = pl.BlockSpec(memory_space=pltpu.SMEM)
    VM = pl.BlockSpec(memory_space=pltpu.VMEM)
    A = pl.BlockSpec(memory_space=pl.ANY)
    resp, stem, gain, tower = pl.pallas_call(
        whole_kernel,
        out_shape=(
            jax.ShapeDtypeStruct((F2, ROWS), BF16),
            jax.ShapeDtypeStruct((K1, 4, C1), F32),
            jax.ShapeDtypeStruct((1, C1), F32),
            jax.ShapeDtypeStruct((K2, 38, C1), F32),
        ),
        in_specs=[VM, S, S, A, VM, VM, A],
        out_specs=(A, VM, VM, VM),
        scratch_shapes=scratch(),
        compiler_params=pltpu.CompilerParams(
            vmem_limit_bytes=62 * 1024 * 1024, collective_id=0, has_side_effects=True
        ),
    )(
        packed, rc_flags, shifts, cotangent[0].T, stem_weight, pool_gain[None],
        jnp.transpose(tower_weight, (1, 0, 2)),
    )
    resp, stem, gain, tower = pl.pallas_call(
        hand_over,
        out_shape=tuple(jax.ShapeDtypeStruct(v.shape, v.dtype) for v in (resp, stem, gain, tower)),
        in_specs=[A] * 4,
        out_specs=(A,) * 4,
        scratch_shapes=[
            pltpu.VMEM((F2, ROWS), BF16),
            pltpu.VMEM((K1, 4, C1), F32),
            pltpu.VMEM((1, C1), F32),
            pltpu.VMEM((K2, 38, C1), F32),
            pltpu.SemaphoreType.DMA((11,)),
            pltpu.SemaphoreType.DMA((11,)),
        ],
        compiler_params=pltpu.CompilerParams(vmem_limit_bytes=60 * 1024 * 1024),
    )(resp, stem, gain, tower)
    return resp.T[None], stem, gain[0], jnp.transpose(tower, (1, 0, 2))


def solution(mesh):
    in_specs = (P("dp", "seq"), P("dp"), P("dp"), P("dp", "seq", None), P(), P(), P())
    out_specs = (P("dp", "seq", None), P(), P(), P("dp", None, None))
    return jax.shard_map(shards, mesh=mesh, in_specs=in_specs, out_specs=out_specs, check_vma=False)
```
